32 devices in a mesh: dp: 4 (over y, x), fsdp: 8 (over z, core).
Axes of the slice: x: 2, y: 2, z: 4, core: 2. Of those that a mesh axis runs over, the one named last changes fastest.
Arguments:
- tokens: bfloat16 [32768, 768], P(('dp', 'fsdp')), may hold values from -6 to 6
- seq_lengths: int32 [32, 9], P(('dp', 'fsdp')), may hold values from 1 to 512, 1024 in all within a row
- query_weight: bfloat16 [768, 768], P(('dp', 'fsdp')), may hold values from -0.21875 to 0.21875
- query_bias: bfloat16 [768], P(('dp', 'fsdp')), may hold values from -3 to 3
- key_weight: bfloat16 [768, 768], P(('dp', 'fsdp')), may hold values from -0.21875 to 0.21875
- value_weight: bfloat16 [768, 768], P(('dp', 'fsdp')), may hold values from -0.21875 to 0.21875
- value_bias: bfloat16 [768], P(('dp', 'fsdp')), may hold values from -0.59765625 to 0.59765625
- out_weight: bfloat16 [768, 768], P(('dp', 'fsdp')), may hold values from -1.75 to 1.75
- out_bias: bfloat16 [768], P(('dp', 'fsdp')), may hold values from -3 to 3
- first_gain: bfloat16 [768], P(('dp', 'fsdp')), may hold values from 0.5 to 1.5
- first_shift: bfloat16 [768], P(('dp', 'fsdp')), may hold values from -3 to 3
- up_weight: bfloat16 [768, 3072], P(('dp', 'fsdp')), may hold values from -0.21875 to 0.21875
- up_bias: bfloat16 [3072], P(('dp', 'fsdp')), may hold values from -3 to 3
- down_weight: bfloat16 [3072, 768], P(('dp', 'fsdp')), may hold values from -0.109375 to 0.109375
- down_bias: bfloat16 [768], P(('dp', 'fsdp')), may hold values from -3 to 3
- second_gain: bfloat16 [768], P(('dp', 'fsdp')), may hold values from 0.5 to 1.5
- second_shift: bfloat16 [768], P(('dp', 'fsdp')), may hold values from -3 to 3
- out_grad: bfloat16 [32768, 768], P(('dp', 'fsdp')), may hold values from -6 to 6
Outputs:
- output: bfloat16 [32768, 768], P(('dp', 'fsdp'))
- tokens_grad: float32 [32768, 768], P(('dp', 'fsdp'))
- grad_query_weight: float32 [768, 768], P(('dp', 'fsdp'))
- grad_query_bias: float32 [768], P(('dp', 'fsdp'))
- grad_key_weight: float32 [768, 768], P(('dp', 'fsdp'))
- grad_value_weight: float32 [768, 768], P(('dp', 'fsdp'))
- grad_value_bias: float32 [768], P(('dp', 'fsdp'))
- grad_out_weight: float32 [768, 768], P(('dp', 'fsdp'))
- grad_out_bias: float32 [768], P(('dp', 'fsdp'))
- grad_first_gain: float32 [768], P(('dp', 'fsdp'))
- grad_first_shift: float32 [768], P(('dp', 'fsdp'))
- grad_up_weight: float32 [768, 3072], P(('dp', 'fsdp'))
- grad_up_bias: float32 [3072], P(('dp', 'fsdp'))
- grad_down_weight: float32 [3072, 768], P(('dp', 'fsdp'))
- grad_down_bias: float32 [768], P(('dp', 'fsdp'))
- grad_second_gain: float32 [768], P(('dp', 'fsdp'))
- grad_second_shift: float32 [768], P(('dp', 'fsdp'))
The draws below stay inside these ranges and needn't reach their ends.
Inputs may be any that keep to these rules, and one draw needn't show every extreme that they name: `seq_lengths`: each row sums to 1024, and its largest entry is exactly 512.
All inputs are finite; a program needn't handle non-finite values.
Results may differ from the reference program's by a relative error of at most 0.014.
Values may be sent and summed in bfloat16 or wider, within the bound.
No kernel may reach another device: no remote copies, remote signals or barrier semaphores. Data moves between devices by JAX's collectives and lax.ppermute only.
A program may use at most 256 MiB of HBM per device.

```python
import math
import jax
import jax.numpy as jnp
import numpy as np
from jax import lax

D = 768
HEADS = 12
FF = 3072
HEAD_DIM = 64
TOK_DEV = 1024
LONGEST = 512
SEQS_DEV = 9
TOKENS = 32768
N_DP = 4
N_FSDP = 8


def raised(entries, own_key, source, target, blocks, factor):
    owner, partner = [(jnp.arange(entries.shape[axis_at]) // (entries.shape[axis_at] // blocks)).reshape([-1 if axis == axis_at else 1 for axis in range(entries.ndim)]) for axis_at in (source, target)]
    chosen = jax.random.permutation(own_key, blocks)[partner]
    strong = (owner == chosen) | (owner == (partner + blocks // 2) % blocks)
    return jnp.where(strong, factor * entries, entries)


def block_levels(rng, shape, cuts, least, top_value):
    level, own = 1.0, jax.random.fold_in(rng, 6)
    for position, blocks in cuts:
        heights = jnp.exp(jax.random.uniform(jax.random.fold_in(own, position), (blocks,), jnp.float32, least / len(cuts), top_value / len(cuts)))
        level = level * jnp.repeat(heights, shape[position] // blocks).reshape([-1 if axis == position else 1 for axis in range(len(shape))])
    return level


def split_up(count, total, limit, slope):
    portions = [(1 << 20) // math.isqrt(standing ** slope) + 1 for standing in range(2, count + 1)]
    spare, counts = total - limit - (count - 1), [1] * (count - 1)
    while spare > 0:
        free = [i for i in range(count - 1) if counts[i] < limit]
        mass, remaining = sum([portions[i] for i in free]), spare
        for i in free:
            more = min(limit - counts[i], max(1, remaining * portions[i] // mass), spare)
            counts[i] = counts[i] + more
            spare = spare - more
    return np.array([limit] + counts)


def uneven(stream_key, number_of, total, most, slope):
    if number_of == 2:
        one = jax.random.randint(stream_key, (), max(1, total - most), min(most, total - 1) + 1)
        return jnp.stack([one, total - one])
    tallies = jnp.asarray(split_up(number_of, total, most, slope), jnp.int32)
    twos = (number_of - 1) // 2
    source_of, taker = tallies[1:1 + 2 * twos:2], tallies[2:2 + 2 * twos:2]
    margin = jnp.minimum(source_of - 1, most - taker)
    shifted = jax.random.randint(jax.random.fold_in(stream_key, 1), (twos,), 0, 1 << 20) % (margin + 1)
    tallies = tallies.at[1:1 + 2 * twos:2].set(source_of - shifted).at[2:2 + 2 * twos:2].set(taker + shifted)
    return tallies[jax.random.permutation(jax.random.fold_in(stream_key, 2), number_of)]


def scatter_about(key, dims, scale, reach, cuts=(), held_as=jnp.bfloat16):
    array = jax.random.normal(key, dims, jnp.float32) * scale
    if len(cuts) > 0:
        array = block_levels(key, dims, cuts, -0.22, 0.18) * array
    return jnp.clip(array, min=-reach, max=reach).astype(held_as)


def noise_with(rng, extent, spread, reach, split, heavy, kind=jnp.bfloat16):
    drawn = spread * jax.random.normal(rng, extent, jnp.float32)
    if split:
        drawn = drawn * block_levels(rng, extent, split, -0.22, 0.18)
    return jnp.clip(raised(drawn, jax.random.fold_in(rng, 3), *heavy), -reach, reach).astype(kind)


def setup_inputs(seed: int = 0) -> dict:
    seeds = jax.random.split(jax.random.key(seed), 19)
    return {
        "tokens": scatter_about(seeds[0], (TOKENS, D), 1.0, 6.0, ((0, 32),)),
        "seq_lengths": jax.vmap(lambda own: uneven(own, SEQS_DEV, TOK_DEV, LONGEST, 2))(jax.random.split(seeds[1], (N_DP * N_FSDP))).reshape((N_DP * N_FSDP, SEQS_DEV)).astype(jnp.int32),
        "query_weight": scatter_about(seeds[2], (D, D), D ** -0.5, 0.21875, ((0, 32),)),
        "query_bias": scatter_about(seeds[3], (D,), 0.5, 3.0, ((0, 32),)),
        "key_weight": scatter_about(seeds[4], (D, D), D ** -0.5, 0.21875, ((0, 32),)),
        "value_weight": scatter_about(seeds[5], (D, D), D ** -0.5, 0.21875, ((0, 32),)),
        "value_bias": scatter_about(seeds[6], (D,), 0.1, 0.59765625, ((0, 32),)),
        "out_weight": scatter_about(seeds[7], (D, D), (D // 64) ** -0.5, 1.75, ((0, 32),)),
        "out_bias": scatter_about(seeds[8], (D,), 0.5, 3.0, ((0, 32),)),
        "first_gain": jnp.clip(1.0 + 0.1 * jax.random.normal(seeds[9], (D,), jnp.float32), 0.5, 1.5).astype(jnp.bfloat16),
        "first_shift": scatter_about(seeds[10], (D,), 0.5, 3.0, ((0, 32),)),
        "up_weight": scatter_about(seeds[11], (D, FF), D ** -0.5, 0.21875, ((0, 32),)),
        "up_bias": scatter_about(seeds[12], (FF,), 0.5, 3.0, ((0, 32),)),
        "down_weight": scatter_about(seeds[13], (FF, D), FF ** -0.5, 0.109375, ((0, 32),)),
        "down_bias": scatter_about(seeds[14], (D,), 0.5, 3.0, ((0, 32),)),
        "second_gain": jnp.clip(1.0 + 0.1 * jax.random.normal(seeds[15], (D,), jnp.float32), 0.5, 1.5).astype(jnp.bfloat16),
        "second_shift": scatter_about(seeds[16], (D,), 0.5, 3.0, ((0, 32),)),
        "out_grad": noise_with(seeds[17], (TOKENS, D), 1.0, 6.0, ((0, 32),), (0, 1, 32, 2.75)),
    }


@jax.custom_vjp
def low(v):
    return lax.optimization_barrier(v.astype(jnp.bfloat16)).astype(jnp.float32)

@jax.custom_vjp
def low_back(v):
    return v

def low_keep(v):
    return (low(v), None)

def low_pass(kept, grad):
    return (grad,)

def back_keep(v):
    return (v, None)

def back_low(kept, grad):
    return (low(grad),)
low.defvjp(low_keep, low_pass)
low_back.defvjp(back_keep, back_low)
EXACT = lax.Precision.HIGHEST
EPSILON = 1e-06
MASKED = -1e+30

def matmul(left, right):
    return jnp.dot(left, right, precision=EXACT, preferred_element_type=jnp.float32)

def round_both(value):
    return low_back(low(value))

def layer_norm(value, gain, shift):
    center = value - lax.optimization_barrier(jnp.mean(value, axis=-1, keepdims=True))
    inverse = lax.rsqrt(lax.optimization_barrier(jnp.mean(center * center, axis=-1, keepdims=True)) + EPSILON)
    return center * inverse * gain + shift

def segment_ids(lengths, row_count):
    seq_ends = jnp.cumsum(lengths)
    positions = jnp.arange(row_count, dtype=jnp.int32)
    return lax.optimization_barrier(jnp.sum((positions[:, None] >= seq_ends[None, :]).astype(jnp.int32), axis=1))

def pack_forward(params, rows, lengths):
    query_mat, query_vec, key_mat, value_mat, value_vec, out_mat, out_vec, gain_one, shift_one, up_mat, up_vec, down_mat, down_vec, gain_two, shift_two = params
    row_count = rows.shape[0]
    segment = segment_ids(lengths, row_count)
    same_seq = segment[:, None] == segment[None, :]
    query_low = round_both(matmul(rows, query_mat) + query_vec).reshape(row_count, HEADS, HEAD_DIM)
    key_low = round_both(matmul(rows, key_mat)).reshape(row_count, HEADS, HEAD_DIM)
    value_low = round_both(matmul(rows, value_mat) + value_vec).reshape(row_count, HEADS, HEAD_DIM)
    scores = low_back(jnp.einsum('qhd,khd->hqk', query_low, key_low, precision=EXACT) * (1.0 / math.sqrt(HEAD_DIM)))
    scores = jnp.where(same_seq[None], scores, MASKED)
    row_max = lax.optimization_barrier(jnp.max(scores, axis=-1, keepdims=True))
    exp_scores = jnp.exp(scores - row_max)
    prob_low = low(exp_scores / lax.optimization_barrier(jnp.sum(exp_scores, axis=-1, keepdims=True)))
    context = jnp.einsum('hqk,khd->qhd', prob_low, value_low, precision=EXACT).reshape(row_count, D)
    context = round_both(context)
    attended = low_back(matmul(context, out_mat) + out_vec)
    middle = layer_norm(rows + attended, gain_one, shift_one)
    middle_low = round_both(middle)
    expand_pre = low_back(matmul(middle_low, up_mat) + up_vec)
    expand_low = low(jax.nn.gelu(expand_pre, approximate=True))
    shrink_out = low_back(matmul(expand_low, down_mat) + down_vec)
    return layer_norm(middle + shrink_out, gain_two, shift_two)

def reference(tokens, seq_lengths, query_weight, query_bias, key_weight, value_weight, value_bias, out_weight, out_bias, first_gain, first_shift, up_weight, up_bias, down_weight, down_bias, second_gain, second_shift, out_grad):
    params = tuple((member.astype(jnp.float32) for member in (query_weight, query_bias, key_weight, value_weight, value_bias, out_weight, out_bias, first_gain, first_shift, up_weight, up_bias, down_weight, down_bias, second_gain, second_shift)))
    packs = tokens.astype(jnp.float32).reshape(N_DP * N_FSDP, TOK_DEV, D)
    forward_step = jax.checkpoint(pack_forward)

    def all_packs(weights, inputs):
        return lax.map(lambda slot_pair: forward_step(weights, slot_pair[0], slot_pair[1]), (inputs, seq_lengths))
    result, pullback = jax.vjp(all_packs, params, packs)
    weight_grads, input_grad = pullback(out_grad.astype(jnp.float32).reshape(N_DP * N_FSDP, TOK_DEV, D))
    output = result.reshape(TOKENS, D).astype(jnp.bfloat16)
    return (output, input_grad.reshape(TOKENS, D), weight_grads[0], weight_grads[1], weight_grads[2], weight_grads[3], weight_grads[4], weight_grads[5], weight_grads[6], weight_grads[7], weight_grads[8], weight_grads[9], weight_grads[10], weight_grads[11], weight_grads[12], weight_grads[13], weight_grads[14])
```

```python
import functools
import math

import jax
import jax.numpy as jnp
from jax import lax
from jax.experimental import pallas as pl
from jax.experimental.pallas import tpu as pltpu
from jax.sharding import PartitionSpec as P

HEAD_DIM = 64
GROUP = 256
PAIR = 128
EPSILON = 1e-06
MASKED = -1e30
LOG2E = 1.4426950408889634
AXES = ("dp", "fsdp")
BF, F32 = jnp.bfloat16, jnp.float32
MIB = 2**20


def dot(a, b, ca=1, cb=0):
    return lax.dot_general(a, b, (((ca,), (cb,)), ((), ())), preferred_element_type=F32)


def call(kernel, cost, vmem=40, **kw):
    return pl.pallas_call(
        kernel,
        compiler_params=pltpu.CompilerParams(vmem_limit_bytes=vmem * MIB),
        cost_estimate=pl.CostEstimate(flops=int(cost * 1e6 * 800), bytes_accessed=0, transcendentals=0),
        **kw,
    )


def seq_ends(len_ref, count):
    ends = [len_ref[0, 0]]
    for j in range(1, count):
        ends.append(ends[-1] + len_ref[0, j])
    return ends


def fill_segments(ends, seg_col, seg_row):
    at_col = lax.broadcasted_iota(jnp.int32, seg_col.shape, 0)
    at_row = lax.broadcasted_iota(jnp.int32, seg_row.shape, 1)
    col, row = jnp.zeros(seg_col.shape, jnp.int32), jnp.zeros(seg_row.shape, jnp.int32)
    for end in ends:
        col = col + (at_col >= end).astype(jnp.int32)
        row = row + (at_row >= end).astype(jnp.int32)
    seg_col[...] = col
    seg_row[...] = row


def key_range(ends, first, last, cases, total):
    low, high = jnp.int32(0), jnp.int32(total)
    for end in ends:
        low = jnp.maximum(low, jnp.where(end <= first, end, 0))
        high = jnp.minimum(high, jnp.where(end > last, end, total))
    start = lax.div(low, 128)
    need = lax.div(high + 127, 128) - start
    case, size = jnp.int32(0), jnp.int32(cases[0])
    for j in range(1, len(cases)):
        more = need > cases[j - 1]
        case = jnp.where(more, j, case)
        size = jnp.where(more, cases[j], size)
    start = jnp.minimum(start, total // 128 - size)
    return pl.multiple_of(start * 128, 128), case


def for_blocks(ends, total, rows_in_block, cases, block):
    cases = tuple(c for c in cases if c < total // 128) + (total // 128,)

    @pl.loop(0, total // rows_in_block)
    def _(i):
        first = i * rows_in_block
        start, case = key_range(ends, first, first + rows_in_block - 1, cases, total)
        for j, n in enumerate(cases):
            pl.when(case == j)(functools.partial(block, pl.multiple_of(first, rows_in_block), n, start))


def attend_kernel(len_ref, tok, w, bias, qkv, ctx, lse, seg_col, seg_row, *, bq, cases, nseq):
    total = tok.shape[0]
    ends = seq_ends(len_ref, nseq)
    fill_segments(ends, seg_col, seg_row)
    for part in range(3):
        cols = pl.ds(part * GROUP, GROUP)
        made = (dot(tok[...], w[:, cols]) + bias[:, cols]).astype(BF)
        qkv[:, cols] = made * BF(1.0 / math.sqrt(HEAD_DIM)) if part == 0 else made

    def block(first, n, start):
        nk = n * 128
        rows, keys = pl.ds(first, bq), pl.ds(start, nk)
        same = jnp.concatenate([seg_col[rows, :]] * n, 1) == seg_row[0:1, keys]
        lane = lax.broadcasted_iota(jnp.int32, (bq, PAIR), 1)
        stats = jnp.zeros((bq, PAIR), F32)
        for pair in range(2):
            q = qkv[rows, pl.ds(pair * PAIR, PAIR)]
            k = qkv[keys, pl.ds(GROUP + pair * PAIR, PAIR)]
            v = qkv[keys, pl.ds(2 * GROUP + pair * PAIR, PAIR)]
            v_ones = jnp.concatenate([v, jnp.ones((nk, PAIR), BF)], 1)
            outs = []
            for h in range(2):
                s = dot(jnp.where((lane < HEAD_DIM) == (h == 0), q, BF(0)), k, 1, 1)
                s = jnp.where(same, s, MASKED)
                top = jnp.max(s, axis=1, keepdims=True)
                o = dot(jnp.exp2((s - top) * LOG2E).astype(BF), v_ones)
                norm = o[:, PAIR:]
                outs.append(o[:, :PAIR] * (1.0 / norm))
                stats = jnp.where(lane == pair * 2 + h, top * LOG2E + jnp.log2(norm), stats)
            ctx[rows, pl.ds(pair * PAIR, PAIR)] = jnp.where(lane < HEAD_DIM, outs[0], outs[1]).astype(BF)
        lse[:, rows] = stats.T[0:8, :]

    for_blocks(ends, total, bq, cases, block)


def attend(lens, tok, w, bias, bq=256, cases=(2, 3, 4, 5, 6)):
    total = tok.shape[0]
    return call(
        functools.partial(attend_kernel, bq=bq, cases=cases, nseq=lens.shape[1]),
        9,
        in_specs=[pl.BlockSpec(memory_space=pltpu.SMEM)] + [pl.BlockSpec(memory_space=pltpu.VMEM)] * 3,
        out_shape=[
            jax.ShapeDtypeStruct((total, 3 * GROUP), BF),
            jax.ShapeDtypeStruct((total, GROUP), BF),
            jax.ShapeDtypeStruct((8, total), F32),
        ],
        scratch_shapes=[pltpu.VMEM((total, 128), jnp.int32), pltpu.VMEM((8, total), jnp.int32)],
        name="attend",
    )(lens, tok, w, bias)


def attend_back_kernel(
    len_ref, tok, w, out_w, qkv, ctx, lse_in, att_back, grad_in, dw, grad_out, sums,
    seg_col, seg_row, key_t, do, dqkv, dk_sum, dv_sum, p_s, ds_s, *, bq, cases, nseq, chunk=2,
):
    total = tok.shape[0]
    ends = seq_ends(len_ref, nseq)
    fill_segments(ends, seg_col, seg_row)
    do[...] = dot(att_back[...], out_w[...], 1, 1).astype(BF)
    key_t[...] = qkv[:, pl.ds(GROUP, GROUP)].T
    dk_sum[...] = jnp.zeros_like(dk_sum)
    dv_sum[...] = jnp.zeros_like(dv_sum)
    head = lax.broadcasted_iota(jnp.int32, (8, GROUP), 1) // HEAD_DIM == lax.broadcasted_iota(jnp.int32, (8, GROUP), 0)
    head = head.astype(BF)

    def block(first, n, start):
        nk = n * 128
        rows, keys = pl.ds(first, bq), pl.ds(start, nk)
        seg_q = seg_row[0:1, rows]
        lane = lax.broadcasted_iota(jnp.int32, (bq, PAIR), 1)
        both = do[rows, :].astype(F32) * ctx[rows, :].astype(F32)
        high = both.astype(BF)
        low = (both - high.astype(F32)).astype(BF)
        delta = dot(head, high, 1, 1) + dot(head, low, 1, 1)
        lse = lse_in[:, rows]
        dqs = []
        for pair in range(2):
            cols = pl.ds(pair * PAIR, PAIR)
            k_cols, v_cols = pl.ds(GROUP + pair * PAIR, PAIR), pl.ds(2 * GROUP + pair * PAIR, PAIR)
            q, g = qkv[rows, cols], do[rows, cols]
            qs, gs = [], []
            for h in range(2):
                head_at = pair * 2 + h
                mine = (lane < HEAD_DIM) == (h == 0)
                qs.append(jnp.where(mine, q, BF(0)))
                gs.append(jnp.where(mine, g, BF(0)))
                for c in range(0, n, chunk):
                    wide = min(chunk, n - c) * 128
                    some = pl.ds(pl.multiple_of(start + c * 128, 128), wide)
                    s = dot(qkv[some, k_cols], qs[h], 1, 1)
                    same = jnp.concatenate([seg_col[some, :]] * (bq // 128), 1) == seg_q
                    p = jnp.exp2(jnp.where(same, s * LOG2E - lse[head_at : head_at + 1, :], MASKED))
                    dp = dot(qkv[some, v_cols], gs[h], 1, 1)
                    p_s[pl.ds(c * 128, wide), pl.ds(h * bq, bq)] = p.astype(BF)
                    ds_s[pl.ds(c * 128, wide), pl.ds(h * bq, bq)] = (p * (dp - delta[head_at : head_at + 1, :])).astype(BF)
            for h in range(2):
                dqs.append(dot(key_t[pl.ds((pair * 2 + h) * HEAD_DIM, HEAD_DIM), keys], ds_s[pl.ds(0, nk), pl.ds(h * bq, bq)]))
            dv_sum[keys, cols] += dot(p_s[pl.ds(0, nk), :], jnp.concatenate(gs, 0))
            dk_sum[keys, cols] += dot(ds_s[pl.ds(0, nk), :], jnp.concatenate(qs, 0))
        dqkv[rows, pl.ds(0, GROUP)] = (jnp.concatenate(dqs, 0).T * (1.0 / math.sqrt(HEAD_DIM))).astype(BF)

    for_blocks(ends, total, bq, cases, block)
    dqkv[:, pl.ds(GROUP, GROUP)] = dk_sum[...].astype(BF)
    dqkv[:, pl.ds(2 * GROUP, GROUP)] = dv_sum[...].astype(BF)
    d = dqkv[...]
    sums[...] = jnp.broadcast_to(jnp.sum(d.astype(F32), axis=0, keepdims=True), sums.shape)
    dw[...] = dot(tok[...], d, 0, 0).astype(BF)
    grad_out[...] = grad_in[...] + dot(d, w[...], 1, 1)


def attend_back(lens, tok, w, out_w, group, qkv, ctx, lse, att_back, grad_in, bq=256, cases=(2, 3, 4, 5, 6)):
    total, width = tok.shape
    vmem = pl.BlockSpec(memory_space=pltpu.VMEM)
    return call(
        functools.partial(attend_back_kernel, bq=bq, cases=cases, nseq=lens.shape[1]),
        12,
        grid=(1,),
        in_specs=[pl.BlockSpec(memory_space=pltpu.SMEM), vmem, vmem, pl.BlockSpec((GROUP, width), lambda _: (group, 0))]
        + [vmem] * 5,
        out_specs=[vmem] * 3,
        out_shape=[
            jax.ShapeDtypeStruct((width, 3 * GROUP), BF),
            jax.ShapeDtypeStruct((total, width), F32),
            jax.ShapeDtypeStruct((8, 3 * GROUP), F32),
        ],
        scratch_shapes=[
            pltpu.VMEM((total, 128), jnp.int32),
            pltpu.VMEM((8, total), jnp.int32),
            pltpu.VMEM((GROUP, total), BF),
            pltpu.VMEM((total, GROUP), BF),
            pltpu.VMEM((total, 3 * GROUP), BF),
            pltpu.VMEM((total, GROUP), F32),
            pltpu.VMEM((total, GROUP), F32),
            pltpu.VMEM((total, 2 * bq), BF),
            pltpu.VMEM((total, 2 * bq), BF),
        ],
        name="attend_back",
    )(lens, tok, w, out_w, qkv, ctx, lse, att_back, grad_in)


def row_mean(value):
    return jnp.sum(value, axis=-1, keepdims=True) * (1.0 / value.shape[-1])


def norm(value):
    center = value - row_mean(value)
    inverse = lax.rsqrt(row_mean(center * center) + EPSILON)
    return center * inverse, inverse


def norm_back(upstream, normed, inverse, gain):
    scaled = upstream * gain
    return inverse * (scaled - row_mean(scaled) - normed * row_mean(scaled * normed))


def add_rows(sums, first, pieces):
    at = lax.broadcasted_iota(jnp.int32, sums.shape, 0)
    made = jnp.zeros(sums.shape, F32)
    for j, piece in enumerate(pieces):
        made = jnp.where(at == j, jnp.sum(piece, axis=0, keepdims=True), made)

    @pl.when(first)
    def _():
        sums[...] = made

    @pl.when(jnp.logical_not(first))
    def _():
        sums[...] += made


def entry_kernel(ctx0, ctx1, ctx2, tok, out_w, vecs, normed, inverse, low):
    ctx = jnp.concatenate([ctx0[...], ctx1[...], ctx2[...]], 1)
    total = tok[...].astype(F32) + (dot(ctx, out_w[...]) + vecs[2:3, :])
    n, r = norm(total)
    normed[...] = n
    inverse[...] = jnp.broadcast_to(r, inverse.shape)
    low[...] = (n * vecs[3:4, :] + vecs[4:5, :]).astype(BF)


def entry(ctxs, tok, out_w, vecs, rows=256):
    total, width = tok.shape
    at = lambda i: (i, 0)
    still = lambda i: (0, 0)
    return call(
        entry_kernel,
        3,
        grid=(total // rows,),
        in_specs=[pl.BlockSpec((rows, GROUP), at)] * 3
        + [pl.BlockSpec((rows, width), at), pl.BlockSpec((width, width), still), pl.BlockSpec(vecs.shape, still)],
        out_specs=[pl.BlockSpec((rows, width), at), pl.BlockSpec((rows, 128), at), pl.BlockSpec((rows, width), at)],
        out_shape=[
            jax.ShapeDtypeStruct((total, width), F32),
            jax.ShapeDtypeStruct((total, 128), F32),
            jax.ShapeDtypeStruct((total, width), BF),
        ],
        name="entry",
    )(*ctxs, tok, out_w, vecs)


ROOT = math.sqrt(2.0 / math.pi)


def expand_kernel(low, up, bias, act, slope, *, rows):
    @pl.loop(0, low.shape[0] // rows)
    def _(i):
        at = pl.ds(pl.multiple_of(i * rows, rows), rows)
        x = dot(low[at, :], up[...]) + bias[...]
        square = x * x
        t = jnp.tanh(x * (ROOT + (ROOT * 0.044715) * square))
        half = 0.5 * x
        act[at, :] = (half + half * t).astype(BF)
        slope[at, :] = (0.5 + 0.5 * t + half * (1.0 - t * t) * (ROOT + (3.0 * ROOT * 0.044715) * square)).astype(BF)


def expand(low, up, bias, wide=512, rows=256):
    total, width = low.shape
    hidden = up.shape[1]
    at = lambda j: (0, j)
    return call(
        functools.partial(expand_kernel, rows=rows),
        7,
        grid=(hidden // wide,),
        in_specs=[pl.BlockSpec((total, width), lambda j: (0, 0)), pl.BlockSpec((width, wide), at), pl.BlockSpec((1, wide), at)],
        out_specs=[pl.BlockSpec((total, wide), at)] * 2,
        out_shape=[jax.ShapeDtypeStruct((total, hidden), BF)] * 2,
        name="expand",
    )(low, up, bias)


def shrink_kernel(act, down, normed, vecs, out_grad, output, back, back_low, sums):
    middle = normed[...] * vecs[3:4, :] + vecs[4:5, :]
    n, r = norm(middle + (dot(act[...], down[...]) + vecs[5:6, :]))
    output[...] = (n * vecs[6:7, :] + vecs[7:8, :]).astype(BF)
    upstream = out_grad[...].astype(F32)
    second = norm_back(upstream, n, r, vecs[6:7, :])
    back[...] = second
    low = second.astype(BF)
    back_low[...] = low
    add_rows(sums, pl.program_id(0) == 0, (upstream * n, upstream, low.astype(F32)))


def shrink(act, down, normed, vecs, out_grad, rows=256):
    total, width = normed.shape
    hidden = act.shape[1]
    at = lambda i: (i, 0)
    still = lambda i: (0, 0)
    block = pl.BlockSpec((rows, width), at)
    return call(
        shrink_kernel,
        7,
        grid=(total // rows,),
        in_specs=[
            pl.BlockSpec((rows, hidden), at),
            pl.BlockSpec((hidden, width), still),
            block,
            pl.BlockSpec(vecs.shape, still),
            block,
        ],
        out_specs=[block, block, block, pl.BlockSpec((8, width), still)],
        out_shape=[
            jax.ShapeDtypeStruct((total, width), BF),
            jax.ShapeDtypeStruct((total, width), F32),
            jax.ShapeDtypeStruct((total, width), BF),
            jax.ShapeDtypeStruct((8, width), F32),
        ],
        name="shrink",
    )(act, down, normed, vecs, out_grad)


def down_grad_kernel(act, back_low, dw):
    dw[...] = dot(act[...], back_low[...], 0, 0).astype(BF)


def down_grad(act, back_low, wide=512):
    total, hidden = act.shape
    width = back_low.shape[1]
    return call(
        down_grad_kernel,
        6,
        grid=(hidden // wide,),
        in_specs=[pl.BlockSpec((total, wide), lambda j: (0, j)), pl.BlockSpec((total, width), lambda j: (0, 0))],
        out_specs=pl.BlockSpec((wide, width), lambda j: (j, 0)),
        out_shape=jax.ShapeDtypeStruct((hidden, width), BF),
        name="down_grad",
    )(act, back_low)


def expand_back_kernel(back_low, down, slope, low, up, dw, back, sums, low_t, ex):
    j = pl.program_id(0)

    @pl.when(j == 0)
    def _():
        low_t[...] = low[...].T
        back[...] = jnp.zeros_like(back)

    ex[...] = (dot(back_low[...], down[...], 1, 1) * slope[...].astype(F32)).astype(BF)
    e = ex[...]
    sums[...] = jnp.broadcast_to(jnp.sum(e.astype(F32), axis=0, keepdims=True), sums.shape)
    dw[...] = dot(low_t[...], e).astype(BF)
    back[...] += dot(e, up[...], 1, 1)


def expand_back(back_low, down, slope, low, up, wide=512):
    total, width = low.shape
    hidden = up.shape[1]
    still = lambda j: (0, 0)
    at = lambda j: (0, j)
    return call(
        expand_back_kernel,
        16,
        grid=(hidden // wide,),
        in_specs=[
            pl.BlockSpec((total, width), still),
            pl.BlockSpec((wide, width), lambda j: (j, 0)),
            pl.BlockSpec((total, wide), at),
            pl.BlockSpec((total, width), still),
            pl.BlockSpec((width, wide), at),
        ],
        out_specs=[pl.BlockSpec((width, wide), at), pl.BlockSpec((total, width), still), pl.BlockSpec((8, wide), at)],
        out_shape=[
            jax.ShapeDtypeStruct((width, hidden), BF),
            jax.ShapeDtypeStruct((total, width), F32),
            jax.ShapeDtypeStruct((8, hidden), F32),
        ],
        scratch_shapes=[pltpu.VMEM((width, total), BF), pltpu.VMEM((total, wide), BF)],
        name="expand_back",
    )(back_low, down, slope, low, up)


def entry_back_kernel(second, expand_part, normed, inverse, ctx0, ctx1, ctx2, vecs, entry_grad, low, dw, sums, *, rows):
    @pl.loop(0, second.shape[0] // rows)
    def _(i):
        at = pl.ds(pl.multiple_of(i * rows, rows), rows)
        upstream = second[at, :] + expand_part[at, :].astype(BF).astype(F32)
        n = normed[at, :]
        made = norm_back(upstream, n, inverse[at, 0:1], vecs[3:4, :])
        entry_grad[at, :] = made
        rounded = made.astype(BF)
        low[at, :] = rounded
        add_rows(sums, i == 0, (upstream * n, upstream, rounded.astype(F32)))

    for g, ctx in enumerate((ctx0, ctx1, ctx2)):
        dw[pl.ds(g * GROUP, GROUP), :] = dot(ctx[...], low[...], 0, 0).astype(BF)


def entry_back(second, expand_part, normed, inverse, ctxs, vecs, rows=128):
    total, width = second.shape
    vmem = pl.BlockSpec(memory_space=pltpu.VMEM)
    return call(
        functools.partial(entry_back_kernel, rows=rows),
        5,
        in_specs=[vmem] * 8,
        out_specs=[vmem] * 4,
        out_shape=[
            jax.ShapeDtypeStruct((total, width), F32),
            jax.ShapeDtypeStruct((total, width), BF),
            jax.ShapeDtypeStruct((width, width), BF),
            jax.ShapeDtypeStruct((8, width), F32),
        ],
        name="entry_back",
    )(second, expand_part, normed, inverse, *ctxs, vecs)


class Cube:
    def __init__(self, mesh):
        self.n_dp, self.n_fsdp = mesh.shape["dp"], mesh.shape["fsdp"]
        self.n = self.n_dp * self.n_fsdp
        self.bits = self.n.bit_length() - 1
        inner = self.n_fsdp.bit_length() - 1
        assert self.n == 1 << self.bits and self.n_fsdp == 1 << inner
        self.near = list(range(1, inner))
        self.far = list(range(inner, self.bits))

    def swap(self, value, bit):
        return lax.ppermute(value, AXES, [(i, i ^ (1 << bit)) for i in range(self.n)])

    def my_bit(self, bit):
        return (lax.axis_index(AXES) >> bit) & 1

    def gather(self, piece, order):
        done = []
        for bit in order:
            other = self.swap(piece, bit)
            at = sum(b > bit for b in done)
            mine_last = self.my_bit(bit) == 1
            piece = jnp.stack([jnp.where(mine_last, other, piece), jnp.where(mine_last, piece, other)], at)
            done.append(bit)
        return piece.reshape(self.n, *piece.shape[self.bits :])

    def scatter(self, whole, order):
        part = whole.reshape((2,) * self.bits + (whole.shape[0] // self.n,) + whole.shape[1:])
        left = list(range(self.bits - 1, -1, -1))
        for bit in order:
            at = left.index(bit)
            left.pop(at)
            mine = self.my_bit(bit)
            keep = lax.dynamic_index_in_dim(part, mine, at, keepdims=False)
            give = lax.dynamic_index_in_dim(part, 1 - mine, at, keepdims=False)
            total = keep.astype(F32) + self.swap(give, bit).astype(F32)
            part = total.astype(BF) if left else total
        return part


def body(cube, *args):
    (
        tokens, seq_lengths, query_weight, query_bias, key_weight, value_weight, value_bias, out_weight, out_bias,
        first_gain, first_shift, up_weight, up_bias, down_weight, down_bias, second_gain, second_shift, out_grad,
    ) = args
    n = cube.n
    width = tokens.shape[1]
    own = width // n
    groups = width // GROUP
    hidden = up_weight.shape[1]
    inward = cube.near[::-1] + cube.far + [0]
    outward = [0] + cube.far + cube.near

    vec_own = jnp.concatenate(
        [query_bias, value_bias, out_bias, first_gain, first_shift, down_bias, second_gain, second_shift, up_bias]
    )
    vec_rows = jnp.pad(vec_own[None], ((0, 7), (0, width - vec_own.shape[0])))
    split = [[m[:, g * GROUP : (g + 1) * GROUP] for g in range(groups)] for m in (query_weight, key_weight, value_weight)]
    packs = [jnp.concatenate([m[g] for m in split], 1) for g in range(groups)]
    first = jnp.concatenate([*packs, vec_rows], 0)
    rest = jnp.concatenate([out_weight, up_weight.reshape(-1, width), down_weight], 0)
    rest_all = lax.all_gather(rest, AXES, axis=0).reshape(n, -1, width)
    first_all = cube.gather(first, inward)
    group_w = [first_all[:, g * own : (g + 1) * own].reshape(width, 3 * GROUP) for g in range(groups)]
    vec_all = first_all[:, groups * own].astype(F32)
    vecs = vec_all[:, : 8 * own].reshape(n, 8, own).transpose(1, 0, 2).reshape(8, width)
    up_b = vec_all[:, 8 * own : 8 * own + hidden // n].reshape(1, hidden)

    zero = jnp.zeros((GROUP,), F32)
    made = []
    for g in range(groups):
        cols = slice(g * GROUP, (g + 1) * GROUP)
        bias = jnp.concatenate([vecs[0, cols], zero, vecs[1, cols]])[None]
        made.append(attend(seq_lengths, tokens, group_w[g], bias))
    ctxs = [m[1] for m in made]
    out_w = rest_all[:, :own].reshape(width, width)
    up = rest_all[:, own : own + own * hidden // width].reshape(width, hidden)
    down = rest_all[:, own + own * hidden // width :].reshape(hidden, width)
    normed, inverse, low = entry(ctxs, tokens, out_w, vecs)
    act, slope = expand(low, up, up_b)
    output, second, back_low, sums_two = shrink(act, down, normed, vecs, out_grad)

    down_dw = down_grad(act, back_low)
    own_down = cube.scatter(down_dw, outward)
    up_dw, expand_part, up_sums = expand_back(back_low, down, slope, low, up)
    own_up = cube.scatter(up_dw, outward)
    grad, att_back, out_dw, sums_one = entry_back(second, expand_part, normed, inverse, ctxs, vecs)
    own_out = cube.scatter(out_dw, outward)
    dws, sums_qkv = [], []
    for g in range(groups):
        qkv, ctx, lse = made[g]
        dw, grad, sums = attend_back(seq_lengths, tokens, group_w[g], out_w, g, qkv, ctx, lse, att_back, grad)
        dws.append(dw.reshape(n, own, 3 * GROUP))
        sums_qkv.append(sums[0])
    query_sum = jnp.concatenate([s[:GROUP] for s in sums_qkv])
    value_sum = jnp.concatenate([s[2 * GROUP :] for s in sums_qkv])
    vec_sums = jnp.stack([query_sum, value_sum, sums_one[2], sums_one[0], sums_one[1], sums_two[2], sums_two[0], sums_two[1]])
    vec_sums = vec_sums.reshape(8, n, own).transpose(1, 0, 2).reshape(n, 8 * own)
    vec_sums = jnp.concatenate([vec_sums, up_sums[0].reshape(n, hidden // n)], 1)
    vec_sums = jnp.pad(vec_sums[:, None], ((0, 0), (0, 7), (0, width - vec_sums.shape[1]))).astype(BF)
    last = jnp.concatenate([*dws, vec_sums], 1)
    own_last = cube.scatter(last.reshape(-1, width), outward)
    own_packs = [own_last[g * own : (g + 1) * own] for g in range(groups)]
    own_q, own_k, own_v = [
        jnp.concatenate([p[:, part * GROUP : (part + 1) * GROUP] for p in own_packs], 1) for part in range(3)
    ]
    own_vec = [own_last[groups * own, j * own : (j + 1) * own] for j in range(8)]
    own_up_b = own_last[groups * own, 8 * own : 8 * own + hidden // n]
    q_b, v_b, out_b, gain_one, shift_one, down_b, gain_two, shift_two = own_vec
    return (
        output, grad, own_q, q_b, own_k, own_v, v_b, own_out, out_b, gain_one, shift_one,
        own_up, own_up_b, own_down, down_b, gain_two, shift_two,
    )


def solution(mesh):
    both = P(AXES)
    rows = P(AXES, None)
    matrix, vector = rows, both
    in_specs = (
        rows, rows, matrix, vector, matrix, matrix, vector, matrix, vector, vector, vector,
        matrix, vector, matrix, vector, vector, vector, rows,
    )
    out_specs = (
        rows, rows, matrix, vector, matrix, matrix, vector, matrix, vector, vector, vector,
        matrix, vector, matrix, vector, vector, vector,
    )
    return jax.shard_map(
        functools.partial(body, Cube(mesh)), mesh=mesh, in_specs=in_specs, out_specs=out_specs, check_vma=False
    )
```

```python
import functools
import math

import jax
import jax.numpy as jnp
from jax import lax
from jax.experimental import pallas as pl
from jax.experimental.pallas import tpu as pltpu
from jax.sharding import PartitionSpec as P

HEAD_DIM = 64
GROUP = 256
PAIR = 128
EPSILON = 1e-06
MASKED = -1e30
LOG2E = 1.4426950408889634
AXES = ("dp", "fsdp")
BF, F32 = jnp.bfloat16, jnp.float32
MIB = 2**20
SCALE = 1
UP_AT_ONCE = False
PLACED = 2**17


def dot(a, b, ca=1, cb=0):
    return lax.dot_general(a, b, (((ca,), (cb,)), ((), ())), preferred_element_type=F32)


def call(kernel, cost, after=(), vmem=40, placed=False, **kw):
    after = tuple(after)
    kw["in_specs"] = list(kw["in_specs"]) + [pl.BlockSpec(memory_space=pl.ANY)] * len(after)
    taken = len(kw["in_specs"]) - len(after)

    def run(*refs):
        kernel(*refs[:taken], *refs[taken + len(after) :])

    made = pl.pallas_call(
        run,
        compiler_params=pltpu.CompilerParams(vmem_limit_bytes=vmem * MIB),
        cost_estimate=pl.CostEstimate(flops=int(cost * 1e6 * SCALE), bytes_accessed=0, transcendentals=0),
        **kw,
    )
    def place(operand):
        small = operand.size * operand.dtype.itemsize < PLACED
        return operand if small or not placed else pltpu.with_memory_space_constraint(operand, pltpu.HBM)

    return lambda *operands: made(*map(place, operands), *after)


def shares(rows, cols, n, dtype=BF):
    own = rows // n
    if own % 8:
        return [jax.ShapeDtypeStruct((rows, cols), dtype)]
    return [jax.ShapeDtypeStruct((n // 2, own, cols), dtype)] * 2


def put_shares(value, core, refs, cols=slice(None)):
    if len(refs) == 1:
        refs[0][:, cols] = value.astype(BF)
        return
    pairs, own = refs[0].shape[:2]
    value = value.reshape(pairs, 2, own, value.shape[-1])
    even, odd = value[:, 0], value[:, 1]
    mine = core == 0
    refs[0][:, :, cols] = jnp.where(mine, even, odd).astype(BF)
    refs[1][:, :, cols] = jnp.where(mine, odd, even).astype(BF)


def seq_ends(len_ref, count):
    ends = [len_ref[0, 0]]
    for j in range(1, count):
        ends.append(ends[-1] + len_ref[0, j])
    return ends


def fill_segments(ends, seg_col, seg_row):
    at_col = lax.broadcasted_iota(jnp.int32, seg_col.shape, 0)
    at_row = lax.broadcasted_iota(jnp.int32, seg_row.shape, 1)
    col, row = jnp.zeros(seg_col.shape, jnp.int32), jnp.zeros(seg_row.shape, jnp.int32)
    for end in ends:
        col = col + (at_col >= end).astype(jnp.int32)
        row = row + (at_row >= end).astype(jnp.int32)
    seg_col[...] = col
    seg_row[...] = row


def key_range(ends, first, last, cases, total):
    low, high = jnp.int32(0), jnp.int32(total)
    for end in ends:
        low = jnp.maximum(low, jnp.where(end <= first, end, 0))
        high = jnp.minimum(high, jnp.where(end > last, end, total))
    start = lax.div(low, 128)
    need = lax.div(high + 127, 128) - start
    case, size = jnp.int32(0), jnp.int32(cases[0])
    for j in range(1, len(cases)):
        more = need > cases[j - 1]
        case = jnp.where(more, j, case)
        size = jnp.where(more, cases[j], size)
    start = jnp.minimum(start, total // 128 - size)
    return pl.multiple_of(start * 128, 128), case


def for_blocks(ends, total, rows_in_block, cases, block):
    cases = tuple(c for c in cases if c < total // 128) + (total // 128,)

    @pl.loop(0, total // rows_in_block)
    def _(i):
        first = i * rows_in_block
        start, case = key_range(ends, first, first + rows_in_block - 1, cases, total)
        for j, n in enumerate(cases):
            pl.when(case == j)(functools.partial(block, pl.multiple_of(first, rows_in_block), n, start))


def attend_kernel(len_ref, tok, w, vecs, qkv, ctx, lse, seg_col, seg_row, *, group, bq, cases, nseq):
    total = tok.shape[0]
    ends = seq_ends(len_ref, nseq)
    fill_segments(ends, seg_col, seg_row)
    for part in range(3):
        cols = pl.ds(part * GROUP, GROUP)
        made = dot(tok[...], w[:, cols])
        if part != 1:
            made = made + vecs[part // 2 : part // 2 + 1, pl.ds(group * GROUP, GROUP)]
        made = made.astype(BF)
        qkv[:, cols] = made * BF(1.0 / math.sqrt(HEAD_DIM)) if part == 0 else made

    def block(first, n, start):
        nk = n * 128
        rows, keys = pl.ds(first, bq), pl.ds(start, nk)
        same = jnp.concatenate([seg_col[rows, :]] * n, 1) == seg_row[0:1, keys]
        lane = lax.broadcasted_iota(jnp.int32, (bq, PAIR), 1)
        stats = jnp.zeros((bq, PAIR), F32)
        for pair in range(2):
            q = qkv[rows, pl.ds(pair * PAIR, PAIR)]
            k = qkv[keys, pl.ds(GROUP + pair * PAIR, PAIR)]
            v = qkv[keys, pl.ds(2 * GROUP + pair * PAIR, PAIR)]
            v_ones = jnp.concatenate([v, jnp.ones((nk, PAIR), BF)], 1)
            outs = []
            for h in range(2):
                s = dot(jnp.where((lane < HEAD_DIM) == (h == 0), q, BF(0)), k, 1, 1)
                s = jnp.where(same, s, MASKED)
                top = jnp.max(s, axis=1, keepdims=True)
                o = dot(jnp.exp2((s - top) * LOG2E).astype(BF), v_ones)
                norm = o[:, PAIR:]
                outs.append(o[:, :PAIR] * (1.0 / norm))
                stats = jnp.where(lane == pair * 2 + h, top * LOG2E + jnp.log2(norm), stats)
            ctx[rows, pl.ds(pair * PAIR, PAIR)] = jnp.where(lane < HEAD_DIM, outs[0], outs[1]).astype(BF)
        lse[:, rows] = stats.T[0:8, :]

    for_blocks(ends, total, bq, cases, block)


def attend(lens, tok, packed, group, vecs, after=(), bq=256, cases=(2, 3, 4, 5, 6)):
    total, width = tok.shape
    vmem = pl.BlockSpec(memory_space=pltpu.VMEM)
    return call(
        functools.partial(attend_kernel, group=group, bq=bq, cases=cases, nseq=lens.shape[1]),
        9,
        after,
        grid=(1,),
        in_specs=[
            pl.BlockSpec(memory_space=pltpu.SMEM),
            vmem,
            pl.BlockSpec((width, 3 * GROUP), lambda _: (0, group)),
            vmem,
        ],
        out_specs=[vmem] * 3,
        out_shape=[
            jax.ShapeDtypeStruct((total, 3 * GROUP), BF),
            jax.ShapeDtypeStruct((total, GROUP), BF),
            jax.ShapeDtypeStruct((8, total), F32),
        ],
        scratch_shapes=[pltpu.VMEM((total, 128), jnp.int32), pltpu.VMEM((8, total), jnp.int32)],
        name="attend",
    )(lens, tok, packed, vecs)


def attend_back_kernel(
    len_ref, core_ref, tok_t, w, out_w, qkv, ctx, lse_in, att_back, grad_in, *refs, extra, carry, n_dw, bq, cases, nseq, chunk=2
):
    extras, carried, refs = refs[:extra], refs[extra : extra + carry], refs[extra + carry :]
    dw, (grad_out, sums) = refs[:n_dw], refs[n_dw : n_dw + 2]
    seg_col, seg_row, key_t, do, dqkv, dk_sum, dv_sum, p_s, ds_s = refs[n_dw + 2 :]
    width, total = tok_t.shape
    ends = seq_ends(len_ref, nseq)
    fill_segments(ends, seg_col, seg_row)
    do[...] = dot(att_back[...], out_w[...], 1, 1).astype(BF)
    key_t[...] = qkv[:, pl.ds(GROUP, GROUP)].T
    dk_sum[...] = jnp.zeros_like(dk_sum)
    dv_sum[...] = jnp.zeros_like(dv_sum)
    head = lax.broadcasted_iota(jnp.int32, (8, GROUP), 1) // HEAD_DIM == lax.broadcasted_iota(jnp.int32, (8, GROUP), 0)
    head = head.astype(BF)

    def block(first, n, start):
        nk = n * 128
        rows, keys = pl.ds(first, bq), pl.ds(start, nk)
        seg_q = seg_row[0:1, rows]
        lane = lax.broadcasted_iota(jnp.int32, (bq, PAIR), 1)
        both = do[rows, :].astype(F32) * ctx[rows, :].astype(F32)
        high = both.astype(BF)
        low = (both - high.astype(F32)).astype(BF)
        delta = dot(head, high, 1, 1) + dot(head, low, 1, 1)
        lse = lse_in[:, rows]
        dqs = []
        for pair in range(2):
            cols = pl.ds(pair * PAIR, PAIR)
            k_cols, v_cols = pl.ds(GROUP + pair * PAIR, PAIR), pl.ds(2 * GROUP + pair * PAIR, PAIR)
            q, g = qkv[rows, cols], do[rows, cols]
            qs, gs = [], []
            for h in range(2):
                head_at = pair * 2 + h
                mine = (lane < HEAD_DIM) == (h == 0)
                qs.append(jnp.where(mine, q, BF(0)))
                gs.append(jnp.where(mine, g, BF(0)))
                for c in range(0, n, chunk):
                    wide = min(chunk, n - c) * 128
                    some = pl.ds(pl.multiple_of(start + c * 128, 128), wide)
                    s = dot(qkv[some, k_cols], qs[h], 1, 1)
                    same = jnp.concatenate([seg_col[some, :]] * (bq // 128), 1) == seg_q
                    p = jnp.exp2(jnp.where(same, s * LOG2E - lse[head_at : head_at + 1, :], MASKED))
                    dp = dot(qkv[some, v_cols], gs[h], 1, 1)
                    p_s[pl.ds(c * 128, wide), pl.ds(h * bq, bq)] = p.astype(BF)
                    ds_s[pl.ds(c * 128, wide), pl.ds(h * bq, bq)] = (p * (dp - delta[head_at : head_at + 1, :])).astype(BF)
            for h in range(2):
                dqs.append(dot(key_t[pl.ds((pair * 2 + h) * HEAD_DIM, HEAD_DIM), keys], ds_s[pl.ds(0, nk), pl.ds(h * bq, bq)]))
            dv_sum[keys, cols] += dot(p_s[pl.ds(0, nk), :], jnp.concatenate(gs, 0))
            dk_sum[keys, cols] += dot(ds_s[pl.ds(0, nk), :], jnp.concatenate(qs, 0))
        dqkv[rows, pl.ds(0, GROUP)] = (jnp.concatenate(dqs, 0).T * (1.0 / math.sqrt(HEAD_DIM))).astype(BF)

    for_blocks(ends, total, bq, cases, block)
    dqkv[:, pl.ds(GROUP, GROUP)] = dk_sum[...].astype(BF)
    dqkv[:, pl.ds(2 * GROUP, GROUP)] = dv_sum[...].astype(BF)
    d = dqkv[...]
    bias_sums = jnp.sum(d.astype(F32), axis=0, keepdims=True)
    sums[...] = jnp.broadcast_to(bias_sums, sums.shape)
    put_shares(dot(tok_t[...], d), core_ref[0, 0], dw, pl.ds(0, 3 * GROUP))
    grad_out[...] = grad_in[...] + dot(d, w[...], 1, 1)
    for source, target in zip(carried, dw):
        target[..., pl.ds(3 * GROUP, width)] = source[...]
    if extra:
        *before, sums_one, sums_two, up_sums = extras
        query = jnp.concatenate([b[0:1, :GROUP] for b in before] + [bias_sums[:, :GROUP]], 1)
        value = jnp.concatenate([b[0:1, 2 * GROUP :] for b in before] + [bias_sums[:, 2 * GROUP :]], 1)
        rows = [query, value, sums_one[2:3], sums_one[0:1], sums_one[1:2], sums_two[2:3], sums_two[0:1], sums_two[1:2]]
        at = lax.broadcasted_iota(jnp.int32, (128, width), 0)
        table = jnp.zeros((128, width), F32)
        for j, row in enumerate([*rows, *(up_sums[j : j + 1] for j in range(4))]):
            table = jnp.where(at == j, row, table)
        put_shares(table.T, core_ref[0, 0], dw, pl.ds(3 * GROUP, 128))


def attend_back(
    lens, core, tok_t, packed, out_up, group, qkv, ctx, lse, att_back, grad_in, n, extras=(), carried=(), after=(), bq=256,
    cases=(2, 3, 4, 5, 6),
):
    width, total = tok_t.shape
    vmem, smem = pl.BlockSpec(memory_space=pltpu.VMEM), pl.BlockSpec(memory_space=pltpu.SMEM)
    dw = shares(width, 3 * GROUP + (128 if extras else 0) + (width if carried else 0), n)
    return call(
        functools.partial(
            attend_back_kernel, extra=len(extras), carry=len(carried), n_dw=len(dw), bq=bq, cases=cases, nseq=lens.shape[1]
        ),
        15,
        after,
        grid=(1,),
        in_specs=[
            smem,
            smem,
            vmem,
            pl.BlockSpec((width, 3 * GROUP), lambda _: (0, group)),
            pl.BlockSpec((GROUP, width), lambda _: (group, 0)),
        ]
        + [vmem] * (5 + len(extras) + len(carried)),
        out_specs=[vmem] * (len(dw) + 2),
        out_shape=[
            *dw,
            jax.ShapeDtypeStruct((total, width), F32),
            jax.ShapeDtypeStruct((8, 3 * GROUP), F32),
        ],
        scratch_shapes=[
            pltpu.VMEM((total, 128), jnp.int32),
            pltpu.VMEM((8, total), jnp.int32),
            pltpu.VMEM((GROUP, total), BF),
            pltpu.VMEM((total, GROUP), BF),
            pltpu.VMEM((total, 3 * GROUP), BF),
            pltpu.VMEM((total, GROUP), F32),
            pltpu.VMEM((total, GROUP), F32),
            pltpu.VMEM((total, 2 * bq), BF),
            pltpu.VMEM((total, 2 * bq), BF),
        ],
        name="attend_back",
    )(lens, core, tok_t, packed, out_up, qkv, ctx, lse, att_back, grad_in, *extras, *carried)


def row_mean(value):
    return jnp.sum(value, axis=-1, keepdims=True) * (1.0 / value.shape[-1])


def norm(value):
    center = value - row_mean(value)
    inverse = lax.rsqrt(row_mean(center * center) + EPSILON)
    return center * inverse, inverse


def norm_back(upstream, normed, inverse, gain):
    scaled = upstream * gain
    return inverse * (scaled - row_mean(scaled) - normed * row_mean(scaled * normed))


def add_rows(sums, first, pieces):
    at = lax.broadcasted_iota(jnp.int32, sums.shape, 0)
    made = jnp.zeros(sums.shape, F32)
    for j, piece in enumerate(pieces):
        made = jnp.where(at == j, jnp.sum(piece, axis=0, keepdims=True), made)

    @pl.when(first)
    def _():
        sums[...] = made

    @pl.when(jnp.logical_not(first))
    def _():
        sums[...] += made


ROOT = math.sqrt(2.0 / math.pi)


def lay_down(core, pieces, whole):
    if len(pieces) == 1:
        whole[...] = pieces[0][...]
        return
    half = len(pieces) // 2
    pairs, each = pieces[0].shape[:2]
    first = 0
    for mine, other in zip(pieces[:half], pieces[half:]):
        cols = pl.ds(first, mine.shape[-1])
        for e in range(pairs):
            a, b = mine[e], other[e]
            whole[pl.ds(2 * e * each, each), cols] = jnp.where(core == 0, a, b)
            whole[pl.ds((2 * e + 1) * each, each), cols] = jnp.where(core == 0, b, a)
        first += mine.shape[-1]


def down_specs(pieces, parts, at):
    if len(pieces) == 1:
        hidden, width = pieces[0].shape
        return [pl.BlockSpec((hidden // parts, width), lambda j: (at(j), 0))]
    return [pl.BlockSpec((p.shape[0] // parts, *p.shape[1:]), lambda j: (at(j), 0, 0)) for p in pieces]


def forward_kernel(core_ref, ctx0, ctx1, ctx2, tok, out_w, up, bias, vecs, out_grad, *refs, rows, parts, n_down, n_dw):
    pieces, dw, refs = refs[:n_down], refs[n_down : n_down + n_dw], refs[n_down + n_dw :]
    output, normed, inverse, low, slope, second, back_low, sums, act, total, down = refs
    j = pl.program_id(0)
    width = tok.shape[1]
    blocks = tok.shape[0] // rows

    @pl.when(j == 0)
    def _():
        @pl.loop(0, blocks)
        def _(i):
            at = pl.ds(pl.multiple_of(i * rows, rows), rows)
            ctx = jnp.concatenate([ctx0[at, :], ctx1[at, :], ctx2[at, :]], 1)
            n, r = norm(tok[at, :].astype(F32) + (dot(ctx, out_w[...]) + vecs[2:3, :]))
            normed[at, :] = n
            inverse[at, :] = jnp.broadcast_to(r, (rows, inverse.shape[1]))
            middle = n * vecs[3:4, :] + vecs[4:5, :]
            low[at, :] = middle.astype(BF)
            total[at, :] = middle + vecs[5:6, :]

    @pl.when(j < parts)
    def _():
        x = dot(low[...], up[...]) + bias[...]
        w = ROOT + (ROOT * 0.044715) * (x * x)
        gate = 0.5 + 0.5 * jnp.tanh(x * w)
        made = x * gate
        slope[...] = (gate + made * (1.0 - gate) * (6.0 * w - 4.0 * ROOT)).astype(BF)
        act[j] = made.astype(BF)
        lay_down(core_ref[0, 0], pieces, down)
        total[...] += dot(act[j], down[...])

    @pl.when(j == parts - 1)
    def _():
        @pl.loop(0, blocks)
        def _(i):
            at = pl.ds(pl.multiple_of(i * rows, rows), rows)
            n, r = norm(total[at, :])
            output[at, :] = (n * vecs[6:7, :] + vecs[7:8, :]).astype(BF)
            upstream = out_grad[at, :].astype(F32)
            made = norm_back(upstream, n, r, vecs[6:7, :])
            second[at, :] = made
            rounded = made.astype(BF)
            back_low[at, :] = rounded
            add_rows(sums, i == 0, (upstream * n, upstream, rounded.astype(F32)))

    @pl.when(j >= parts)
    def _():
        put_shares(dot(act[j - parts], back_low[...], 0, 0), core_ref[0, 0], dw)


def forward(core, ctxs, tok, out_up, up_bias, down, vecs, out_grad, n, rows=256):
    total, width = tok.shape
    hidden = up_bias.shape[1]
    parts = hidden // width
    vmem = pl.BlockSpec(memory_space=pltpu.VMEM)
    first = lambda j: jnp.minimum(j, parts - 1)
    last = lambda j: jnp.maximum(j - parts, 0)
    dw = shares(hidden, width, n)
    return call(
        functools.partial(forward_kernel, rows=rows, parts=parts, n_down=len(down), n_dw=len(dw)),
        32,
        vmem=48,
        placed=True,
        grid=(2 * parts,),
        in_specs=[pl.BlockSpec(memory_space=pltpu.SMEM)]
        + [vmem] * 4
        + [
            pl.BlockSpec((width, width), lambda j: (0, 0)),
            pl.BlockSpec((width, width), lambda j: (0, first(j) + 1)),
            pl.BlockSpec((1, width), lambda j: (0, first(j))),
            vmem,
            vmem,
            *down_specs(down, parts, first),
        ],
        out_specs=down_specs(dw, parts, last)
        + [vmem] * 4
        + [pl.BlockSpec((total, width), lambda j: (0, first(j))), vmem, vmem, vmem],
        out_shape=[
            *dw,
            jax.ShapeDtypeStruct((total, width), BF),
            jax.ShapeDtypeStruct((total, width), F32),
            jax.ShapeDtypeStruct((total, 128), F32),
            jax.ShapeDtypeStruct((total, width), BF),
            jax.ShapeDtypeStruct((total, hidden), BF),
            jax.ShapeDtypeStruct((total, width), F32),
            jax.ShapeDtypeStruct((total, width), BF),
            jax.ShapeDtypeStruct((8, width), F32),
        ],
        scratch_shapes=[
            pltpu.VMEM((parts, total, width), BF),
            pltpu.VMEM((total, width), F32),
            pltpu.VMEM((width, width), BF),
        ],
        name="forward",
    )(core, *ctxs, tok, out_up, out_up, up_bias, vecs, out_grad, *down)


def backward_kernel(
    core_ref, back_low, slope, low, up, second, normed, inverse, ctx0, ctx1, ctx2, vecs, *refs, rows, n_dw, n_down
):
    pieces, refs = refs[:n_down], refs[n_down:]
    dw, out_dw, refs = refs[: n_dw[0]], refs[n_dw[0] : sum(n_dw)], refs[sum(n_dw) :]
    up_sums, entry_grad, att_back, sums, low_t, back, ex, down = refs
    j = pl.program_id(0)
    blocks = low.shape[0] // rows

    @pl.when(j == 0)
    def _():
        low_t[...] = low[...].T
        back[...] = jnp.zeros_like(back)

    lay_down(core_ref[0, 0], pieces, down)
    ex[...] = (dot(back_low[...], down[...], 1, 1) * slope[...].astype(F32)).astype(BF)
    up_sums[...] = jnp.broadcast_to(jnp.sum(ex[...].astype(F32), axis=0, keepdims=True), up_sums.shape)
    back[...] += dot(ex[...], up[...], 1, 1)
    put_shares(dot(low_t[...], ex[...]), core_ref[0, 0], dw)

    @pl.when(j == pl.num_programs(0) - 1)
    def _():
        @pl.loop(0, blocks)
        def _(i):
            at = pl.ds(pl.multiple_of(i * rows, rows), rows)
            upstream = second[at, :] + back[at, :].astype(BF).astype(F32)
            n = normed[at, :]
            made = norm_back(upstream, n, inverse[at, 0:1], vecs[3:4, :])
            entry_grad[at, :] = made
            rounded = made.astype(BF)
            att_back[at, :] = rounded
            add_rows(sums, i == 0, (upstream * n, upstream, rounded.astype(F32)))

        ctx = jnp.concatenate([ctx0[...], ctx1[...], ctx2[...]], 1)
        put_shares(dot(ctx, att_back[...], 0, 0), core_ref[0, 0], out_dw)


def backward(core, back_low, down, slope, low, out_up, second, normed, inverse, ctxs, vecs, n, after=(), rows=256):
    total, width = low.shape
    hidden = slope.shape[1]
    vmem = pl.BlockSpec(memory_space=pltpu.VMEM)
    dw = [jax.ShapeDtypeStruct((width, hidden), BF)] if UP_AT_ONCE else shares(width, hidden, n)
    out_dw = shares(width, width, n)
    lead = (0,) * (len(dw[0].shape) - 1)
    return call(
        functools.partial(backward_kernel, rows=rows, n_dw=(len(dw), len(out_dw)), n_down=len(down)),
        26,
        after,
        vmem=44,
        placed=True,
        grid=(hidden // width,),
        in_specs=[
            pl.BlockSpec(memory_space=pltpu.SMEM),
            vmem,
            pl.BlockSpec((total, width), lambda j: (0, j)),
            vmem,
            pl.BlockSpec((width, width), lambda j: (0, j + 1)),
        ]
        + [vmem] * 7
        + down_specs(down, hidden // width, lambda j: j),
        out_specs=[pl.BlockSpec((*d.shape[:-1], width), lambda j: (*lead, j)) for d in dw]
        + [vmem] * len(out_dw)
        + [pl.BlockSpec((8, width), lambda j: (0, j))]
        + [vmem] * 3,
        out_shape=[
            *dw,
            *out_dw,
            jax.ShapeDtypeStruct((8, hidden), F32),
            jax.ShapeDtypeStruct((total, width), F32),
            jax.ShapeDtypeStruct((total, width), BF),
            jax.ShapeDtypeStruct((8, width), F32),
        ],
        scratch_shapes=[
            pltpu.VMEM((width, total), BF),
            pltpu.VMEM((total, width), F32),
            pltpu.VMEM((total, width), BF),
            pltpu.VMEM((width, width), BF),
        ],
        name="backward",
    )(core, back_low, slope, low, out_up, second, normed, inverse, *ctxs, vecs, *down)


def pack_kernel(query, key, value, table, packed):
    own, width = query.shape
    for g in range(width // GROUP):
        for part, matrix in enumerate((query, key, value)):
            packed[:, pl.ds((3 * g + part) * GROUP, GROUP)] = matrix[:, pl.ds(g * GROUP, GROUP)]
    packed[:, pl.ds(3 * width, 128)] = table[...].astype(F32).T[:own, :].astype(BF)


def pack(query, key, value, rows):
    own, width = query.shape
    table = jnp.pad(rows, ((0, 128 - rows.shape[0]), (0, 128 - own)))
    vmem = pl.BlockSpec(memory_space=pltpu.VMEM)
    return call(
        pack_kernel,
        1,
        in_specs=[vmem] * 4,
        out_specs=vmem,
        out_shape=jax.ShapeDtypeStruct((own, 3 * width + 128), BF),
        name="pack",
    )(query, key, value, table)


def turn_kernel(packed, vecs):
    vecs[...] = packed[...].astype(F32).T[: vecs.shape[0], :]


def turn(packed, first):
    width = packed.shape[0]
    return call(
        turn_kernel,
        1,
        grid=(1,),
        in_specs=[pl.BlockSpec((width, 128), lambda _: (0, first // 128))],
        out_specs=pl.BlockSpec(memory_space=pltpu.VMEM),
        out_shape=jax.ShapeDtypeStruct((16, width), F32),
        name="turn",
    )(packed)


class Cube:
    def __init__(self, mesh):
        self.n_dp, self.n_fsdp = mesh.shape["dp"], mesh.shape["fsdp"]
        self.n = self.n_dp * self.n_fsdp
        self.bits = self.n.bit_length() - 1
        inner = self.n_fsdp.bit_length() - 1
        assert self.n == 1 << self.bits and self.n_fsdp == 1 << inner
        self.near = list(range(1, inner))
        self.far = list(range(inner, self.bits))

    def swap(self, value, bit):
        return lax.ppermute(value, AXES, [(i, i ^ (1 << bit)) for i in range(self.n)])

    def my_bit(self, bit):
        return (lax.axis_index(AXES) >> bit) & 1

    def join(self, mine, other, bit, done):
        at = sum(b > bit for b in done)
        last = self.my_bit(bit) == 1
        return jnp.stack([jnp.where(last, other, mine), jnp.where(last, mine, other)], at)

    def gather_near(self, piece, step, done):
        bit = self.near[::-1][step]
        return self.join(piece, self.swap(piece, bit), bit, done), [*done, bit]

    def halve(self, piece):
        half = piece.shape[-1] // 256 * 128
        return [piece[..., :half], piece[..., half:]]

    def gather_far(self, parts, step, done):
        orders = [self.far[::-1], self.far[:1] + self.far[:0:-1]]
        bits = [order[step] for order in orders]
        before = [[*done, *order[:step]] for order in orders]
        return [self.join(p, self.swap(p, bit), bit, d) for p, bit, d in zip(parts, bits, before)]

    def gather_core(self, parts, others):
        done = self.near + self.far
        whole = jnp.concatenate([self.join(p, o, 0, done) for p, o in zip(parts, others)], -1)
        return whole.reshape(-1, whole.shape[-1])

    def fold(self, part, left, bit):
        at = left.index(bit)
        rest = left[:at] + left[at + 1 :]
        mine = self.my_bit(bit)
        keep = lax.dynamic_index_in_dim(part, mine, at, keepdims=False)
        give = lax.dynamic_index_in_dim(part, 1 - mine, at, keepdims=False)
        total = keep.astype(F32) + self.swap(give, bit).astype(F32)
        return (total.astype(BF) if rest else total), rest

    def scatter_core(self, given):
        left = list(range(self.bits - 1, -1, -1))
        if len(given) == 2:
            keep, give = given
            part = (keep.astype(F32) + self.swap(give, 0).astype(F32)).astype(BF)
            part = part.reshape((2,) * (self.bits - 1) + part.shape[1:])
        else:
            whole = given[0].reshape((2,) * self.bits + (-1, given[0].shape[-1]))
            part, _ = self.fold(whole, left, 0)
        return part

    def scatter_far(self, parts, step):
        made = []
        for part, order in zip(parts, (self.far, self.far[1:] + self.far[:1])):
            left = [b for b in range(self.bits - 1, 0, -1) if b not in order[:step]]
            made.append(self.fold(part, left, order[step])[0])
        return made


class Flow:
    def __init__(self, cube, parts):
        self.cube, self.parts, self.left = cube, list(parts), list(range(cube.bits - 1, 0, -1))
        self.todo = [("far", i) for i in range(len(cube.far))] + [("near", bit) for bit in cube.near]

    def step(self, *after):
        if not self.todo:
            return
        (where, i), *self.todo = self.todo
        parts = [tie(p, *after) for p in self.parts] if after else self.parts
        if where == "far":
            self.parts = self.cube.scatter_far(parts, i)
        else:
            part = jnp.concatenate(parts, -1) if len(parts) > 1 else parts[0]
            left = [b for b in self.cube.near if b >= i][::-1]
            self.parts = [self.cube.fold(part, left, i)[0]]

    def finish(self):
        while self.todo:
            self.step()
        return self.parts[0]


def tie(value, *others):
    return lax.optimization_barrier((value, *others))[0]


def body(cube, *args):
    (
        tokens, seq_lengths, query_weight, query_bias, key_weight, value_weight, value_bias, out_weight, out_bias,
        first_gain, first_shift, up_weight, up_bias, down_weight, down_bias, second_gain, second_shift, out_grad,
    ) = args
    n = cube.n
    width = tokens.shape[1]
    own = width // n
    groups = width // GROUP
    hidden = up_weight.shape[1]
    each = hidden // width
    core = cube.my_bit(0).astype(jnp.int32).reshape(1, 1)

    vectors = (query_bias, value_bias, out_bias, first_gain, first_shift, down_bias, second_gain, second_shift)
    rows = jnp.concatenate([jnp.stack(vectors), up_bias.reshape(each, own)])
    piece, done = pack(query_weight, key_weight, value_weight, rows), []
    out_up = lax.all_gather(jnp.concatenate([out_weight, up_weight], 1), AXES, axis=0, tiled=True)
    down_piece, down_done = down_weight, []
    steps_near, steps_far = len(cube.near), len(cube.far)
    for step in range(steps_near):
        piece, done = cube.gather_near(piece, step, done)
    parts = cube.halve(piece)
    for step in range(max(steps_far, steps_near)):
        if step < steps_near:
            down_piece = tie(down_piece, *parts)
        if step < steps_far:
            parts = cube.gather_far(parts, step, done)
        if step < steps_near:
            down_piece, down_done = cube.gather_near(down_piece, step, down_done)
    packed = cube.gather_core(parts, [cube.swap(p, 0) for p in parts])
    vecs = turn(packed, 3 * GROUP * groups)
    up_b = vecs[8 : 8 + each].reshape(each, n, own).transpose(1, 0, 2).reshape(1, hidden)
    tok_t = tokens.T

    down_parts = [tie(p, packed) for p in cube.halve(down_piece)]
    made, wait = [], [tok_t, up_b]
    for g in range(groups):
        if g < steps_far:
            down_parts = cube.gather_far(down_parts, g, down_done)
        made.append(attend(seq_lengths, tokens, packed, g, vecs, wait))
        wait = [made[-1][2], *down_parts]
        down_parts = [tie(p, made[-1][2]) for p in down_parts] if g < steps_far else down_parts
    for step in range(groups, steps_far):
        down_parts = cube.gather_far(down_parts, step, down_done)
    ctxs = [m[1] for m in made]
    down_others = [cube.swap(p, 0) for p in down_parts]
    if hidden // n % 16:
        down = [cube.gather_core(down_parts, down_others)]
    else:
        down = [p.reshape(-1, *p.shape[-2:]) for p in (*down_parts, *down_others)]
    *down_dw, output, normed, inverse, low, slope, second, back_low, sums_two = forward(
        core, ctxs, tokens, out_up, up_b, down, vecs, out_grad, n
    )
    flows = [Flow(cube, cube.halve(cube.scatter_core(down_dw)))]

    *dws, up_sums, grad, att_back, sums_one = backward(
        core, back_low, down, slope, low, out_up, second, normed, inverse, ctxs, vecs, n
    )
    half = 1 if UP_AT_ONCE else len(dws) // 2
    out_dw = dws[half:]
    wait = flows[0].parts
    flows[0].step(sums_one)
    if UP_AT_ONCE:
        own_up = lax.psum_scatter(dws[0], AXES, scatter_dimension=0, tiled=True).astype(F32)
    else:
        flows.append(Flow(cube, cube.halve(cube.scatter_core(dws[:half]))))
    up_sums = up_sums[0].reshape(width, each).T
    later, sums_qkv = [], []
    for g in range(groups):
        qkv, ctx, lse = made[g]
        extras = (*sums_qkv, sums_one, sums_two, up_sums) if g == groups - 1 else ()
        *dw, grad, sums = attend_back(
            seq_lengths, core, tok_t, packed, out_up, g, qkv, ctx, lse, att_back, grad, n, extras, out_dw if g == 0 else (),
            wait,
        )
        sums_qkv.append(sums)
        wait = [p for flow in flows for p in flow.parts]
        for flow in flows:
            flow.step(sums)
        if g == 0:
            flows.append(Flow(cube, cube.halve(cube.scatter_core(dw))))
        else:
            later.append(cube.scatter_core(dw))
    own_down, *own_up_too, first = [flow.finish() for flow in flows]
    if own_up_too:
        (own_up,) = own_up_too
    both = Flow(cube, later).finish()
    owned = [first]
    owned += [both[:, g * 3 * GROUP : (g + 1) * 3 * GROUP + (128 if g == groups - 2 else 0)] for g in range(groups - 1)]
    own_out = owned[0][:, 3 * GROUP :]
    own_q, own_k, own_v = [
        jnp.concatenate([p[:, part * GROUP : (part + 1) * GROUP] for p in owned], 1) for part in range(3)
    ]
    own_vec = owned[-1][:, 3 * GROUP :]
    q_b, v_b, out_b, gain_one, shift_one, down_b, gain_two, shift_two = [own_vec[:, j] for j in range(8)]
    own_up_b = own_vec[:, 8 : 8 + each].reshape(-1)
    return (
        output, grad, own_q, q_b, own_k, own_v, v_b, own_out, out_b, gain_one, shift_one,
        own_up, own_up_b, own_down, down_b, gain_two, shift_two,
    )


def solution(mesh):
    both = P(AXES)
    rows = P(AXES, None)
    matrix, vector = rows, both
    in_specs = (
        rows, rows, matrix, vector, matrix, matrix, vector, matrix, vector, vector, vector,
        matrix, vector, matrix, vector, vector, vector, rows,
    )
    out_specs = (
        rows, rows, matrix, vector, matrix, matrix, vector, matrix, vector, vector, vector,
        matrix, vector, matrix, vector, vector, vector,
    )
    return jax.shard_map(
        functools.partial(body, Cube(mesh)), mesh=mesh, in_specs=in_specs, out_specs=out_specs, check_vma=False
    )
```

```python
import functools
import math

import jax
import jax.numpy as jnp
from jax import lax
from jax.experimental import pallas as pl
from jax.experimental.pallas import tpu as pltpu
from jax.sharding import PartitionSpec as P

HEAD_DIM = 64
GROUP = 256
PAIR = 128
EPSILON = 1e-06
MASKED = -1e30
LOG2E = 1.4426950408889634
AXES = ("dp", "fsdp")
BF, F32 = jnp.bfloat16, jnp.float32
MIB = 2**20
SCALE = 1
PLACED = 2**17


def dot(a, b, ca=1, cb=0):
    return lax.dot_general(a, b, (((ca,), (cb,)), ((), ())), preferred_element_type=F32)


def large(array):
    return math.prod(array.shape) * jnp.dtype(array.dtype).itemsize >= PLACED


def call(kernel, cost, after=(), vmem=40, placed=False, pinned=False, **kw):
    after = tuple(after)
    kw["in_specs"] = list(kw["in_specs"]) + [pl.BlockSpec(memory_space=pl.ANY)] * len(after)
    taken = len(kw["in_specs"]) - len(after)

    if pinned:
        kw["out_shape"] = [pltpu.HBM(s.shape, s.dtype) if large(s) else s for s in kw["out_shape"]]

    def run(*refs):
        kernel(*refs[:taken], *refs[taken + len(after) :])

    made = pl.pallas_call(
        run,
        compiler_params=pltpu.CompilerParams(vmem_limit_bytes=vmem * MIB),
        cost_estimate=pl.CostEstimate(flops=int(cost * 1e6 * SCALE), bytes_accessed=0, transcendentals=0),
        **kw,
    )
    def place(operand):
        return operand if not placed or not large(operand) else pltpu.with_memory_space_constraint(operand, pltpu.HBM)

    return lambda *operands: made(*map(place, operands), *after)


def shares(rows, cols, n, dtype=BF):
    own = rows // n
    if own % 8:
        return [jax.ShapeDtypeStruct((rows, cols), dtype)]
    return [jax.ShapeDtypeStruct((n // 2, own, cols), dtype)] * 2


def put_shares(value, core, refs, cols=slice(None)):
    if len(refs) == 1:
        refs[0][:, cols] = value.astype(BF)
        return
    pairs, own = refs[0].shape[:2]
    value = value.reshape(pairs, 2, own, value.shape[-1])
    even, odd = value[:, 0], value[:, 1]
    mine = core == 0
    refs[0][:, :, cols] = jnp.where(mine, even, odd).astype(BF)
    refs[1][:, :, cols] = jnp.where(mine, odd, even).astype(BF)


def seq_ends(len_ref, count):
    ends = [len_ref[0, 0]]
    for j in range(1, count):
        ends.append(ends[-1] + len_ref[0, j])
    return ends


def fill_segments(ends, seg_col, seg_row):
    at_col = lax.broadcasted_iota(jnp.int32, seg_col.shape, 0)
    at_row = lax.broadcasted_iota(jnp.int32, seg_row.shape, 1)
    col, row = jnp.zeros(seg_col.shape, jnp.int32), jnp.zeros(seg_row.shape, jnp.int32)
    for end in ends:
        col = col + (at_col >= end).astype(jnp.int32)
        row = row + (at_row >= end).astype(jnp.int32)
    seg_col[...] = col
    seg_row[...] = row


def key_range(ends, first, last, cases, total):
    low, high = jnp.int32(0), jnp.int32(total)
    for end in ends:
        low = jnp.maximum(low, jnp.where(end <= first, end, 0))
        high = jnp.minimum(high, jnp.where(end > last, end, total))
    start = lax.div(low, 128)
    need = lax.div(high + 127, 128) - start
    case, size = jnp.int32(0), jnp.int32(cases[0])
    for j in range(1, len(cases)):
        more = need > cases[j - 1]
        case = jnp.where(more, j, case)
        size = jnp.where(more, cases[j], size)
    start = jnp.minimum(start, total // 128 - size)
    return pl.multiple_of(start * 128, 128), case


def for_blocks(ends, total, rows_in_block, cases, block):
    cases = tuple(c for c in cases if c < total // 128) + (total // 128,)

    @pl.loop(0, total // rows_in_block)
    def _(i):
        first = i * rows_in_block
        start, case = key_range(ends, first, first + rows_in_block - 1, cases, total)
        for j, n in enumerate(cases):
            pl.when(case == j)(functools.partial(block, pl.multiple_of(first, rows_in_block), n, start))


def attend_kernel(len_ref, tok, w, vecs, qkv, ctx, lse, seg_col, seg_row, *, group, bq, cases, nseq):
    total = tok.shape[0]
    ends = seq_ends(len_ref, nseq)
    fill_segments(ends, seg_col, seg_row)
    for part in range(3):
        cols = pl.ds(part * GROUP, GROUP)
        made = dot(tok[...], w[:, cols])
        if part != 1:
            made = made + vecs[part // 2 : part // 2 + 1, pl.ds(group * GROUP, GROUP)]
        made = made.astype(BF)
        qkv[:, cols] = made * BF(1.0 / math.sqrt(HEAD_DIM)) if part == 0 else made

    def block(first, n, start):
        nk = n * 128
        rows, keys = pl.ds(first, bq), pl.ds(start, nk)
        same = jnp.concatenate([seg_col[rows, :]] * n, 1) == seg_row[0:1, keys]
        lane = lax.broadcasted_iota(jnp.int32, (bq, PAIR), 1)
        stats = jnp.zeros((bq, PAIR), F32)
        for pair in range(2):
            q = qkv[rows, pl.ds(pair * PAIR, PAIR)]
            k = qkv[keys, pl.ds(GROUP + pair * PAIR, PAIR)]
            v = qkv[keys, pl.ds(2 * GROUP + pair * PAIR, PAIR)]
            v_ones = jnp.concatenate([v, jnp.ones((nk, PAIR), BF)], 1)
            outs = []
            for h in range(2):
                s = dot(jnp.where((lane < HEAD_DIM) == (h == 0), q, BF(0)), k, 1, 1)
                s = jnp.where(same, s, MASKED)
                top = jnp.max(s, axis=1, keepdims=True)
                o = dot(jnp.exp2((s - top) * LOG2E).astype(BF), v_ones)
                norm = o[:, PAIR:]
                outs.append(o[:, :PAIR] * (1.0 / norm))
                stats = jnp.where(lane == pair * 2 + h, top * LOG2E + jnp.log2(norm), stats)
            ctx[rows, pl.ds(pair * PAIR, PAIR)] = jnp.where(lane < HEAD_DIM, outs[0], outs[1]).astype(BF)
        lse[:, rows] = stats.T[0:8, :]

    for_blocks(ends, total, bq, cases, block)


def attend(lens, tok, packed, group, vecs, after=(), bq=256, cases=(2, 3, 4, 5, 6)):
    total, width = tok.shape
    vmem = pl.BlockSpec(memory_space=pltpu.VMEM)
    return call(
        functools.partial(attend_kernel, group=group, bq=bq, cases=cases, nseq=lens.shape[1]),
        9,
        after,
        grid=(1,),
        in_specs=[
            pl.BlockSpec(memory_space=pltpu.SMEM),
            vmem,
            pl.BlockSpec((width, 3 * GROUP), lambda _: (0, group)),
            vmem,
        ],
        out_specs=[vmem] * 3,
        out_shape=[
            jax.ShapeDtypeStruct((total, 3 * GROUP), BF),
            jax.ShapeDtypeStruct((total, GROUP), BF),
            jax.ShapeDtypeStruct((8, total), F32),
        ],
        scratch_shapes=[pltpu.VMEM((total, 128), jnp.int32), pltpu.VMEM((8, total), jnp.int32)],
        name="attend",
    )(lens, tok, packed, vecs)


def attend_back_kernel(
    len_ref, core_ref, tok_t, out_w, qkv, ctx, lse_in, att_back, *refs, extra, carry, n_dw, bq, cases, nseq, chunk=2
):
    extras, carried, refs = refs[:extra], refs[extra : extra + carry], refs[extra + carry :]
    dw, (dqkv, sums) = refs[:n_dw], refs[n_dw : n_dw + 2]
    seg_col, seg_row, key_t, do, dk_sum, dv_sum, p_s, ds_s = refs[n_dw + 2 :]
    width, total = tok_t.shape
    ends = seq_ends(len_ref, nseq)
    fill_segments(ends, seg_col, seg_row)
    do[...] = dot(att_back[...], out_w[...], 1, 1).astype(BF)
    key_t[...] = qkv[:, pl.ds(GROUP, GROUP)].T
    dk_sum[...] = jnp.zeros_like(dk_sum)
    dv_sum[...] = jnp.zeros_like(dv_sum)
    head = lax.broadcasted_iota(jnp.int32, (8, GROUP), 1) // HEAD_DIM == lax.broadcasted_iota(jnp.int32, (8, GROUP), 0)
    head = head.astype(BF)

    def block(first, n, start):
        nk = n * 128
        rows, keys = pl.ds(first, bq), pl.ds(start, nk)
        seg_q = seg_row[0:1, rows]
        lane = lax.broadcasted_iota(jnp.int32, (bq, PAIR), 1)
        both = do[rows, :].astype(F32) * ctx[rows, :].astype(F32)
        high = both.astype(BF)
        low = (both - high.astype(F32)).astype(BF)
        delta = dot(head, high, 1, 1) + dot(head, low, 1, 1)
        lse = lse_in[:, rows]
        dqs = []
        for pair in range(2):
            cols = pl.ds(pair * PAIR, PAIR)
            k_cols, v_cols = pl.ds(GROUP + pair * PAIR, PAIR), pl.ds(2 * GROUP + pair * PAIR, PAIR)
            q, g = qkv[rows, cols], do[rows, cols]
            qs, gs = [], []
            for h in range(2):
                head_at = pair * 2 + h
                mine = (lane < HEAD_DIM) == (h == 0)
                qs.append(jnp.where(mine, q, BF(0)))
                gs.append(jnp.where(mine, g, BF(0)))
                for c in range(0, n, chunk):
                    wide = min(chunk, n - c) * 128
                    some = pl.ds(pl.multiple_of(start + c * 128, 128), wide)
                    s = dot(qkv[some, k_cols], qs[h], 1, 1)
                    same = jnp.concatenate([seg_col[some, :]] * (bq // 128), 1) == seg_q
                    p = jnp.exp2(jnp.where(same, s * LOG2E - lse[head_at : head_at + 1, :], MASKED))
                    dp = dot(qkv[some, v_cols], gs[h], 1, 1)
                    p_s[pl.ds(c * 128, wide), pl.ds(h * bq, bq)] = p.astype(BF)
                    ds_s[pl.ds(c * 128, wide), pl.ds(h * bq, bq)] = (p * (dp - delta[head_at : head_at + 1, :])).astype(BF)
            for h in range(2):
                dqs.append(dot(key_t[pl.ds((pair * 2 + h) * HEAD_DIM, HEAD_DIM), keys], ds_s[pl.ds(0, nk), pl.ds(h * bq, bq)]))
            dv_sum[keys, cols] += dot(p_s[pl.ds(0, nk), :], jnp.concatenate(gs, 0))
            dk_sum[keys, cols] += dot(ds_s[pl.ds(0, nk), :], jnp.concatenate(qs, 0))
        dqkv[rows, pl.ds(0, GROUP)] = (jnp.concatenate(dqs, 0).T * (1.0 / math.sqrt(HEAD_DIM))).astype(BF)

    for_blocks(ends, total, bq, cases, block)
    dqkv[:, pl.ds(GROUP, GROUP)] = dk_sum[...].astype(BF)
    dqkv[:, pl.ds(2 * GROUP, GROUP)] = dv_sum[...].astype(BF)
    d = dqkv[...]
    bias_sums = jnp.sum(d.astype(F32), axis=0, keepdims=True)
    sums[...] = jnp.broadcast_to(bias_sums, sums.shape)
    put_shares(dot(tok_t[...], d), core_ref[0, 0], dw, pl.ds(0, 3 * GROUP))
    for source, target in zip(carried, dw):
        target[..., pl.ds(3 * GROUP, width)] = source[...]
    if extra:
        *before, sums_one, sums_two, up_sums = extras
        query = jnp.concatenate([b[0:1, :GROUP] for b in before] + [bias_sums[:, :GROUP]], 1)
        value = jnp.concatenate([b[0:1, 2 * GROUP :] for b in before] + [bias_sums[:, 2 * GROUP :]], 1)
        rows = [query, value, sums_one[2:3], sums_one[0:1], sums_one[1:2], sums_two[2:3], sums_two[0:1], sums_two[1:2]]
        at = lax.broadcasted_iota(jnp.int32, (128, width), 0)
        table = jnp.zeros((128, width), F32)
        for j, row in enumerate([*rows, *(up_sums[j : j + 1] for j in range(4))]):
            table = jnp.where(at == j, row, table)
        put_shares(table.T, core_ref[0, 0], dw, pl.ds(3 * GROUP, 128))


def attend_back(
    lens, core, tok_t, out_up, group, qkv, ctx, lse, att_back, n, extras=(), carried=(), after=(), bq=256,
    cases=(2, 3, 4, 5, 6),
):
    width, total = tok_t.shape
    vmem, smem = pl.BlockSpec(memory_space=pltpu.VMEM), pl.BlockSpec(memory_space=pltpu.SMEM)
    dw = shares(width, 3 * GROUP + (128 if extras else 0) + (width if carried else 0), n)
    return call(
        functools.partial(
            attend_back_kernel, extra=len(extras), carry=len(carried), n_dw=len(dw), bq=bq, cases=cases, nseq=lens.shape[1]
        ),
        15,
        after,
        pinned=True,
        grid=(1,),
        in_specs=[
            smem,
            smem,
            vmem,
            pl.BlockSpec((GROUP, width), lambda _: (group, 0)),
        ]
        + [vmem] * (4 + len(extras) + len(carried)),
        out_specs=[vmem] * (len(dw) + 2),
        out_shape=[
            *dw,
            jax.ShapeDtypeStruct((total, 3 * GROUP), BF),
            jax.ShapeDtypeStruct((8, 3 * GROUP), F32),
        ],
        scratch_shapes=[
            pltpu.VMEM((total, 128), jnp.int32),
            pltpu.VMEM((8, total), jnp.int32),
            pltpu.VMEM((GROUP, total), BF),
            pltpu.VMEM((total, GROUP), BF),
            pltpu.VMEM((total, GROUP), F32),
            pltpu.VMEM((total, GROUP), F32),
            pltpu.VMEM((total, 2 * bq), BF),
            pltpu.VMEM((total, 2 * bq), BF),
        ],
        name="attend_back",
    )(lens, core, tok_t, out_up, qkv, ctx, lse, att_back, *extras, *carried)


def tokens_back_kernel(grad_in, w, *refs):
    *ds, grad = refs
    d = jnp.concatenate([r[...] for r in ds], 1)
    grad[...] = grad_in[...] + dot(d, w[:, : d.shape[1]], 1, 1)


def tokens_back(grad, packed, ds, after=(), rows=256):
    total, width = grad.shape
    at = lambda i: (i, 0)
    return call(
        tokens_back_kernel,
        8,
        after,
        placed=True,
        grid=(total // rows,),
        in_specs=[pl.BlockSpec((rows, width), at), pl.BlockSpec(packed.shape, lambda i: (0, 0))]
        + [pl.BlockSpec((rows, 3 * GROUP), at)] * len(ds),
        out_specs=pl.BlockSpec((rows, width), at),
        out_shape=jax.ShapeDtypeStruct((total, width), F32),
        name="tokens_back",
    )(grad, packed, *ds)


def row_mean(value):
    return jnp.sum(value, axis=-1, keepdims=True) * (1.0 / value.shape[-1])


def norm(value):
    center = value - row_mean(value)
    inverse = lax.rsqrt(row_mean(center * center) + EPSILON)
    return center * inverse, inverse


def norm_back(upstream, normed, inverse, gain):
    scaled = upstream * gain
    return inverse * (scaled - row_mean(scaled) - normed * row_mean(scaled * normed))


def add_rows(sums, first, pieces):
    at = lax.broadcasted_iota(jnp.int32, sums.shape, 0)
    made = jnp.zeros(sums.shape, F32)
    for j, piece in enumerate(pieces):
        made = jnp.where(at == j, jnp.sum(piece, axis=0, keepdims=True), made)

    @pl.when(first)
    def _():
        sums[...] = made

    @pl.when(jnp.logical_not(first))
    def _():
        sums[...] += made


ROOT = math.sqrt(2.0 / math.pi)


def lay_down(core, pieces, whole):
    if len(pieces) == 1:
        whole[...] = pieces[0][...]
        return
    half = len(pieces) // 2
    pairs, each = pieces[0].shape[:2]
    first = 0
    for mine, other in zip(pieces[:half], pieces[half:]):
        cols = pl.ds(first, mine.shape[-1])
        for e in range(pairs):
            a, b = mine[e], other[e]
            whole[pl.ds(2 * e * each, each), cols] = jnp.where(core == 0, a, b)
            whole[pl.ds((2 * e + 1) * each, each), cols] = jnp.where(core == 0, b, a)
        first += mine.shape[-1]


def down_specs(pieces, parts, at):
    if len(pieces) == 1:
        hidden, width = pieces[0].shape
        return [pl.BlockSpec((hidden // parts, width), lambda j: (at(j), 0))]
    return [pl.BlockSpec((p.shape[0] // parts, *p.shape[1:]), lambda j: (at(j), 0, 0)) for p in pieces]


def forward_kernel(core_ref, ctx0, ctx1, ctx2, tok, out_w, up, bias, vecs, out_grad_far, *refs, rows, parts, n_down, n_dw):
    pieces, dw, refs = refs[:n_down], refs[n_down : n_down + n_dw], refs[n_down + n_dw :]
    far, (slope, sums, act, total, down), near, (out_grad, sems) = refs[:6], refs[6:11], refs[11:17], refs[17:]
    normed, inverse, low, output, second, back_low = near
    bring = pltpu.make_async_copy(out_grad_far, out_grad, sems.at[6])
    take = [pltpu.make_async_copy(near[i], far[i], sems.at[i]) for i in range(6)]
    j = pl.program_id(0)
    width = tok.shape[1]
    blocks = tok.shape[0] // rows

    @pl.when(j == 0)
    def _():
        bring.start()

        @pl.loop(0, blocks)
        def _(i):
            at = pl.ds(pl.multiple_of(i * rows, rows), rows)
            ctx = jnp.concatenate([ctx0[at, :], ctx1[at, :], ctx2[at, :]], 1)
            n, r = norm(tok[at, :].astype(F32) + (dot(ctx, out_w[...]) + vecs[2:3, :]))
            normed[at, :] = n
            inverse[at, :] = jnp.broadcast_to(r, (rows, inverse.shape[1]))
            middle = n * vecs[3:4, :] + vecs[4:5, :]
            low[at, :] = middle.astype(BF)
            total[at, :] = middle + vecs[5:6, :]

        for copy in take[:3]:
            copy.start()

    @pl.when(j < parts)
    def _():
        x = dot(low[...], up[...]) + bias[...]
        w = ROOT + (ROOT * 0.044715) * (x * x)
        gate = 0.5 + 0.5 * jnp.tanh(x * w)
        made = x * gate
        slope[...] = (gate + made * (1.0 - gate) * (6.0 * w - 4.0 * ROOT)).astype(BF)
        act[j] = made.astype(BF)
        lay_down(core_ref[0, 0], pieces, down)
        total[...] += dot(act[j], down[...])

    @pl.when(j == parts - 1)
    def _():
        bring.wait()

        @pl.loop(0, blocks)
        def _(i):
            at = pl.ds(pl.multiple_of(i * rows, rows), rows)
            n, r = norm(total[at, :])
            output[at, :] = (n * vecs[6:7, :] + vecs[7:8, :]).astype(BF)
            upstream = out_grad[at, :].astype(F32)
            made = norm_back(upstream, n, r, vecs[6:7, :])
            second[at, :] = made
            rounded = made.astype(BF)
            back_low[at, :] = rounded
            add_rows(sums, i == 0, (upstream * n, upstream, rounded.astype(F32)))

        for copy in take[3:]:
            copy.start()

    @pl.when(j >= parts)
    def _():
        put_shares(dot(act[j - parts], back_low[...], 0, 0), core_ref[0, 0], dw)

    @pl.when(j == 2 * parts - 1)
    def _():
        for copy in take:
            copy.wait()


def forward(core, ctxs, tok, out_up, up_bias, down, vecs, out_grad, n, rows=256):
    total, width = tok.shape
    hidden = up_bias.shape[1]
    parts = hidden // width
    vmem = pl.BlockSpec(memory_space=pltpu.VMEM)
    first = lambda j: jnp.minimum(j, parts - 1)
    last = lambda j: jnp.maximum(j - parts, 0)
    dw = shares(hidden, width, n)
    hbm = pl.BlockSpec(memory_space=pl.ANY)
    wide = (total, width)
    kept = [(wide, F32), ((total, 128), F32), (wide, BF), (wide, BF), (wide, F32), (wide, BF)]
    return call(
        functools.partial(forward_kernel, rows=rows, parts=parts, n_down=len(down), n_dw=len(dw)),
        32,
        vmem=48,
        placed=True,
        pinned=True,
        grid=(2 * parts,),
        in_specs=[pl.BlockSpec(memory_space=pltpu.SMEM)]
        + [vmem] * 4
        + [
            pl.BlockSpec((width, width), lambda j: (0, 0)),
            pl.BlockSpec((width, width), lambda j: (0, first(j) + 1)),
            pl.BlockSpec((1, width), lambda j: (0, first(j))),
            vmem,
            hbm,
            *down_specs(down, parts, first),
        ],
        out_specs=down_specs(dw, parts, last)
        + [hbm] * len(kept)
        + [pl.BlockSpec((total, width), lambda j: (0, first(j))), vmem],
        out_shape=[
            *dw,
            *(jax.ShapeDtypeStruct(*k) for k in kept),
            jax.ShapeDtypeStruct((total, hidden), BF),
            jax.ShapeDtypeStruct((8, width), F32),
        ],
        scratch_shapes=[
            pltpu.VMEM((parts, total, width), BF),
            pltpu.VMEM((total, width), F32),
            pltpu.VMEM((width, width), BF),
            *(pltpu.VMEM(*k) for k in kept),
            pltpu.VMEM((total, width), BF),
            pltpu.SemaphoreType.DMA((7,)),
        ],
        name="forward",
    )(core, *ctxs, tok, out_up, out_up, up_bias, vecs, out_grad, *down)


def backward_kernel(
    core_ref, back_low, slope, low, up, vecs, *refs, rows, n_dw, n_down
):
    far, pieces, refs = refs[:6], refs[6 : 6 + n_down], refs[6 + n_down :]
    dw, out_dw, refs = refs[: n_dw[0]], refs[n_dw[0] : sum(n_dw)], refs[sum(n_dw) :]
    (up_sums, sums), out_far, (low_t, back, ex, down), near, (entry_grad, att_back, sems) = (
        refs[:2], refs[2:4], refs[4:8], refs[8:14], refs[14:]
    )
    second, normed, inverse, ctx0, ctx1, ctx2 = near
    bring = [pltpu.make_async_copy(far[i], near[i], sems.at[i]) for i in range(6)]
    take = [pltpu.make_async_copy(a, b, sems.at[6 + i]) for i, (a, b) in enumerate(zip((entry_grad, att_back), out_far))]
    j = pl.program_id(0)
    blocks = low.shape[0] // rows

    @pl.when(j == 0)
    def _():
        for copy in bring:
            copy.start()
        low_t[...] = low[...].T
        back[...] = jnp.zeros_like(back)

    lay_down(core_ref[0, 0], pieces, down)
    ex[...] = (dot(back_low[...], down[...], 1, 1) * slope[...].astype(F32)).astype(BF)
    up_sums[...] = jnp.broadcast_to(jnp.sum(ex[...].astype(F32), axis=0, keepdims=True), up_sums.shape)
    back[...] += dot(ex[...], up[...], 1, 1)
    put_shares(dot(low_t[...], ex[...]), core_ref[0, 0], dw)

    @pl.when(j == pl.num_programs(0) - 1)
    def _():
        for copy in bring:
            copy.wait()

        @pl.loop(0, blocks)
        def _(i):
            at = pl.ds(pl.multiple_of(i * rows, rows), rows)
            upstream = second[at, :] + back[at, :].astype(BF).astype(F32)
            n = normed[at, :]
            made = norm_back(upstream, n, inverse[at, 0:1], vecs[3:4, :])
            entry_grad[at, :] = made
            rounded = made.astype(BF)
            att_back[at, :] = rounded
            add_rows(sums, i == 0, (upstream * n, upstream, rounded.astype(F32)))

        for copy in take:
            copy.start()
        ctx = jnp.concatenate([ctx0[...], ctx1[...], ctx2[...]], 1)
        put_shares(dot(ctx, att_back[...], 0, 0), core_ref[0, 0], out_dw)
        for copy in take:
            copy.wait()


def backward(core, back_low, down, slope, low, out_up, second, normed, inverse, ctxs, vecs, n, after=(), rows=256):
    total, width = low.shape
    hidden = slope.shape[1]
    vmem = pl.BlockSpec(memory_space=pltpu.VMEM)
    dw, out_dw = shares(width, hidden, n), shares(width, width, n)
    hbm = pl.BlockSpec(memory_space=pl.ANY)
    lead = (0,) * (len(dw[0].shape) - 1)
    return call(
        functools.partial(backward_kernel, rows=rows, n_dw=(len(dw), len(out_dw)), n_down=len(down)),
        26,
        after,
        vmem=44,
        placed=True,
        pinned=True,
        grid=(hidden // width,),
        in_specs=[
            pl.BlockSpec(memory_space=pltpu.SMEM),
            vmem,
            pl.BlockSpec((total, width), lambda j: (0, j)),
            vmem,
            pl.BlockSpec((width, width), lambda j: (0, j + 1)),
            vmem,
        ]
        + [hbm] * 6
        + down_specs(down, hidden // width, lambda j: j),
        out_specs=[pl.BlockSpec((*d.shape[:-1], width), lambda j: (*lead, j)) for d in dw]
        + [vmem] * len(out_dw)
        + [pl.BlockSpec((8, width), lambda j: (0, j)), vmem, hbm, hbm],
        out_shape=[
            *dw,
            *out_dw,
            jax.ShapeDtypeStruct((8, hidden), F32),
            jax.ShapeDtypeStruct((8, width), F32),
            jax.ShapeDtypeStruct((total, width), F32),
            jax.ShapeDtypeStruct((total, width), BF),
        ],
        scratch_shapes=[
            pltpu.VMEM((width, total), BF),
            pltpu.VMEM((total, width), F32),
            pltpu.VMEM((total, width), BF),
            pltpu.VMEM((width, width), BF),
            pltpu.VMEM((total, width), F32),
            pltpu.VMEM((total, width), F32),
            pltpu.VMEM((total, 128), F32),
            *[pltpu.VMEM((total, GROUP), BF)] * 3,
            pltpu.VMEM((total, width), F32),
            pltpu.VMEM((total, width), BF),
            pltpu.SemaphoreType.DMA((8,)),
        ],
        name="backward",
    )(core, back_low, slope, low, out_up, vecs, second, normed, inverse, *ctxs, *down)


def pack_kernel(query, key, value, table, packed):
    own, width = query.shape
    for g in range(width // GROUP):
        for part, matrix in enumerate((query, key, value)):
            packed[:, pl.ds((3 * g + part) * GROUP, GROUP)] = matrix[:, pl.ds(g * GROUP, GROUP)]
    packed[:, pl.ds(3 * width, 128)] = table[...].astype(F32).T[:own, :].astype(BF)


def pack(query, key, value, rows):
    own, width = query.shape
    table = jnp.pad(rows, ((0, 128 - rows.shape[0]), (0, 128 - own)))
    vmem = pl.BlockSpec(memory_space=pltpu.VMEM)
    return call(
        pack_kernel,
        1,
        in_specs=[vmem] * 4,
        out_specs=vmem,
        out_shape=jax.ShapeDtypeStruct((own, 3 * width + 128), BF),
        name="pack",
    )(query, key, value, table)


def turn_kernel(packed, vecs):
    vecs[...] = packed[...].astype(F32).T[: vecs.shape[0], :]


def turn(packed, first):
    width = packed.shape[0]
    return call(
        turn_kernel,
        1,
        grid=(1,),
        in_specs=[pl.BlockSpec((width, 128), lambda _: (0, first // 128))],
        out_specs=pl.BlockSpec(memory_space=pltpu.VMEM),
        out_shape=jax.ShapeDtypeStruct((16, width), F32),
        name="turn",
    )(packed)


class Cube:
    def __init__(self, mesh):
        self.n_dp, self.n_fsdp = mesh.shape["dp"], mesh.shape["fsdp"]
        self.n = self.n_dp * self.n_fsdp
        self.bits = self.n.bit_length() - 1
        inner = self.n_fsdp.bit_length() - 1
        assert self.n == 1 << self.bits and self.n_fsdp == 1 << inner
        self.near = list(range(1, inner))
        self.far = list(range(inner, self.bits))

    def swap(self, value, bit):
        return lax.ppermute(value, AXES, [(i, i ^ (1 << bit)) for i in range(self.n)])

    def my_bit(self, bit):
        return (lax.axis_index(AXES) >> bit) & 1

    def join(self, mine, other, bit, done):
        at = sum(b > bit for b in done)
        last = self.my_bit(bit) == 1
        return jnp.stack([jnp.where(last, other, mine), jnp.where(last, mine, other)], at)

    def gather_near(self, piece, step, done):
        bit = self.near[::-1][step]
        return self.join(piece, self.swap(piece, bit), bit, done), [*done, bit]

    def halve(self, piece):
        half = piece.shape[-1] // 256 * 128
        return [piece[..., :half], piece[..., half:]]

    def gather_far(self, parts, step, done):
        orders = [self.far[::-1], self.far[:1] + self.far[:0:-1]]
        bits = [order[step] for order in orders]
        before = [[*done, *order[:step]] for order in orders]
        return [self.join(p, self.swap(p, bit), bit, d) for p, bit, d in zip(parts, bits, before)]

    def gather_core(self, parts, others):
        done = self.near + self.far
        whole = jnp.concatenate([self.join(p, o, 0, done) for p, o in zip(parts, others)], -1)
        return whole.reshape(-1, whole.shape[-1])

    def fold(self, part, left, bit):
        at = left.index(bit)
        rest = left[:at] + left[at + 1 :]
        mine = self.my_bit(bit)
        keep = lax.dynamic_index_in_dim(part, mine, at, keepdims=False)
        give = lax.dynamic_index_in_dim(part, 1 - mine, at, keepdims=False)
        total = keep.astype(F32) + self.swap(give, bit).astype(F32)
        return (total.astype(BF) if rest else total), rest

    def scatter_core(self, given):
        left = list(range(self.bits - 1, -1, -1))
        if len(given) == 2:
            keep, give = given
            part = (keep.astype(F32) + self.swap(give, 0).astype(F32)).astype(BF)
            part = part.reshape((2,) * (self.bits - 1) + part.shape[1:])
        else:
            whole = given[0].reshape((2,) * self.bits + (-1, given[0].shape[-1]))
            part, _ = self.fold(whole, left, 0)
        return part

    def scatter_far(self, parts, step):
        made = []
        for part, order in zip(parts, (self.far, self.far[1:] + self.far[:1])):
            left = [b for b in range(self.bits - 1, 0, -1) if b not in order[:step]]
            made.append(self.fold(part, left, order[step])[0])
        return made


class Flow:
    def __init__(self, cube, parts):
        self.cube, self.parts, self.left = cube, list(parts), list(range(cube.bits - 1, 0, -1))
        self.todo = [("far", i) for i in range(len(cube.far))] + [("near", bit) for bit in cube.near]

    def step(self, *after):
        if not self.todo:
            return
        (where, i), *self.todo = self.todo
        parts = [tie(p, *after) for p in self.parts] if after else self.parts
        if where == "far":
            self.parts = self.cube.scatter_far(parts, i)
        else:
            part = jnp.concatenate(parts, -1) if len(parts) > 1 else parts[0]
            left = [b for b in self.cube.near if b >= i][::-1]
            self.parts = [self.cube.fold(part, left, i)[0]]

    def finish(self):
        while self.todo:
            self.step()
        return self.parts[0]


def tie(value, *others):
    return lax.optimization_barrier((value, *others))[0]


def body(cube, *args):
    (
        tokens, seq_lengths, query_weight, query_bias, key_weight, value_weight, value_bias, out_weight, out_bias,
        first_gain, first_shift, up_weight, up_bias, down_weight, down_bias, second_gain, second_shift, out_grad,
    ) = args
    n = cube.n
    width = tokens.shape[1]
    own = width // n
    groups = width // GROUP
    hidden = up_weight.shape[1]
    each = hidden // width
    core = cube.my_bit(0).astype(jnp.int32).reshape(1, 1)

    vectors = (query_bias, value_bias, out_bias, first_gain, first_shift, down_bias, second_gain, second_shift)
    rows = jnp.concatenate([jnp.stack(vectors), up_bias.reshape(each, own)])
    piece, done = pack(query_weight, key_weight, value_weight, rows), []
    out_up = lax.all_gather(jnp.concatenate([out_weight, up_weight], 1), AXES, axis=0, tiled=True)
    down_piece, down_done = down_weight, []
    steps_near, steps_far = len(cube.near), len(cube.far)
    for step in range(steps_near):
        piece, done = cube.gather_near(piece, step, done)
    parts = cube.halve(piece)
    tok_t = tie(tokens, piece).T
    for step in range(max(steps_far, steps_near)):
        if step < steps_near:
            down_piece = tie(down_piece, *parts)
        if step < steps_far:
            parts = cube.gather_far(parts, step, done)
        if step < steps_near:
            down_piece, down_done = cube.gather_near(down_piece, step, down_done)
    packed = cube.gather_core(parts, [cube.swap(p, 0) for p in parts])
    vecs = turn(packed, 3 * GROUP * groups)
    up_b = vecs[8 : 8 + each].reshape(each, n, own).transpose(1, 0, 2).reshape(1, hidden)

    down_parts = [tie(p, packed) for p in cube.halve(down_piece)]
    made, wait = [], [tok_t, up_b]
    for g in range(groups):
        if g < steps_far:
            down_parts = cube.gather_far(down_parts, g, down_done)
        made.append(attend(seq_lengths, tokens, packed, g, vecs, wait))
        wait = [made[-1][2], *down_parts]
        down_parts = [tie(p, made[-1][2]) for p in down_parts] if g < steps_far else down_parts
    for step in range(groups, steps_far):
        down_parts = cube.gather_far(down_parts, step, down_done)
    ctxs = [m[1] for m in made]
    down_others = [cube.swap(p, 0) for p in down_parts]
    if hidden // n % 16:
        down = [cube.gather_core(down_parts, down_others)]
    else:
        down = [p.reshape(-1, *p.shape[-2:]) for p in (*down_parts, *down_others)]
    *down_dw, normed, inverse, low, output, second, back_low, slope, sums_two = forward(
        core, ctxs, tokens, out_up, up_b, down, vecs, out_grad, n
    )
    down_flow = Flow(cube, cube.halve(cube.scatter_core(down_dw)))

    *dws, up_sums, sums_one, grad, att_back = backward(
        core, back_low, down, slope, low, out_up, second, normed, inverse, ctxs, vecs, n
    )
    half = len(dws) // 2
    out_dw = dws[half:]
    up_sums = up_sums[0].reshape(width, each).T
    wait = down_flow.parts
    down_flow.step(sums_one)
    flows = [down_flow, Flow(cube, cube.halve(cube.scatter_core(dws[:half])))]
    later, sums_qkv, ds = [], [], []
    for g in range(groups):
        qkv, ctx, lse = made[g]
        extras = (*sums_qkv, sums_one, sums_two, up_sums) if g == groups - 1 else ()
        *dw, d, sums = attend_back(
            seq_lengths, core, tok_t, out_up, g, qkv, ctx, lse, att_back, n, extras, out_dw if g == 0 else (), wait
        )
        ds.append(d)
        sums_qkv.append(sums)
        wait = [p for flow in flows for p in flow.parts]
        if g < groups - 1:
            for flow in flows:
                flow.step(sums)
        if g == groups - 1:
            dw = [tie(p, *(p for flow in flows for p in flow.parts)) for p in dw]
        if g == 0:
            flows.append(Flow(cube, [cube.scatter_core(dw)]))
        else:
            later.append(cube.scatter_core(dw))
    both = Flow(cube, later)
    grad = tokens_back(grad, packed, ds, later[-1:])
    while both.todo or any(flow.todo for flow in flows):
        before = [p for flow in (both, *flows) for p in flow.parts]
        for flow in (both, *flows):
            flow.step(*before)
    own_down, own_up, first = [flow.parts[0] for flow in flows]
    both = both.parts[0]
    owned = [first]
    owned += [both[:, g * 3 * GROUP : (g + 1) * 3 * GROUP + (128 if g == groups - 2 else 0)] for g in range(groups - 1)]
    own_out = owned[0][:, 3 * GROUP :]
    own_q, own_k, own_v = [
        jnp.concatenate([p[:, part * GROUP : (part + 1) * GROUP] for p in owned], 1) for part in range(3)
    ]
    own_vec = owned[-1][:, 3 * GROUP :]
    q_b, v_b, out_b, gain_one, shift_one, down_b, gain_two, shift_two = [own_vec[:, j] for j in range(8)]
    own_up_b = own_vec[:, 8 : 8 + each].reshape(-1)
    return (
        output, grad, own_q, q_b, own_k, own_v, v_b, own_out, out_b, gain_one, shift_one,
        own_up, own_up_b, own_down, down_b, gain_two, shift_two,
    )


def solution(mesh):
    both = P(AXES)
    rows = P(AXES, None)
    matrix, vector = rows, both
    in_specs = (
        rows, rows, matrix, vector, matrix, matrix, vector, matrix, vector, vector, vector,
        matrix, vector, matrix, vector, vector, vector, rows,
    )
    out_specs = (
        rows, rows, matrix, vector, matrix, matrix, vector, matrix, vector, vector, vector,
        matrix, vector, matrix, vector, vector, vector,
    )
    return jax.shard_map(
        functools.partial(body, Cube(mesh)), mesh=mesh, in_specs=in_specs, out_specs=out_specs, check_vma=False
    )
```

```python
import functools
import math

import jax
import jax.numpy as jnp
from jax import lax
from jax.experimental import pallas as pl
from jax.experimental.pallas import tpu as pltpu
from jax.sharding import PartitionSpec as P

HEAD_DIM = 64
GROUP = 256
PAIR = 128
EPSILON = 1e-06
MASKED = -1e30
LOG2E = 1.4426950408889634
AXES = ("dp", "fsdp")
BF, F32 = jnp.bfloat16, jnp.float32
MIB = 2**20
SCALE = 1
PLACED = 2**17


def dot(a, b, ca=1, cb=0):
    return lax.dot_general(a, b, (((ca,), (cb,)), ((), ())), preferred_element_type=F32)


def large(array):
    return math.prod(array.shape) * jnp.dtype(array.dtype).itemsize >= PLACED


def call(kernel, cost, after=(), vmem=40, placed=False, pinned=False, **kw):
    after = tuple(after)
    kw["in_specs"] = list(kw["in_specs"]) + [pl.BlockSpec(memory_space=pl.ANY)] * len(after)
    taken = len(kw["in_specs"]) - len(after)

    if pinned:
        kw["out_shape"] = [pltpu.HBM(s.shape, s.dtype) if large(s) else s for s in kw["out_shape"]]

    def run(*refs):
        kernel(*refs[:taken], *refs[taken + len(after) :])

    made = pl.pallas_call(
        run,
        compiler_params=pltpu.CompilerParams(vmem_limit_bytes=vmem * MIB),
        cost_estimate=pl.CostEstimate(flops=int(cost * 1e6 * SCALE), bytes_accessed=0, transcendentals=0),
        **kw,
    )
    def place(operand):
        return operand if not placed or not large(operand) else pltpu.with_memory_space_constraint(operand, pltpu.HBM)

    return lambda *operands: made(*map(place, operands), *after)


def shares(rows, cols, n, dtype=BF):
    own = rows // n
    if own % 8:
        return [jax.ShapeDtypeStruct((rows, cols), dtype)]
    return [jax.ShapeDtypeStruct((n // 2, own, cols), dtype)] * 2


def put_shares(value, core, refs, cols=slice(None)):
    if len(refs) == 1:
        refs[0][:, cols] = value.astype(BF)
        return
    pairs, own = refs[0].shape[:2]
    value = value.reshape(pairs, 2, own, value.shape[-1])
    even, odd = value[:, 0], value[:, 1]
    mine = core == 0
    refs[0][:, :, cols] = jnp.where(mine, even, odd).astype(BF)
    refs[1][:, :, cols] = jnp.where(mine, odd, even).astype(BF)


def seq_ends(len_ref, count):
    ends = [len_ref[0, 0]]
    for j in range(1, count):
        ends.append(ends[-1] + len_ref[0, j])
    return ends


def fill_segments(ends, seg_col, seg_row):
    at_col = lax.broadcasted_iota(jnp.int32, seg_col.shape, 0)
    at_row = lax.broadcasted_iota(jnp.int32, seg_row.shape, 1)
    col, row = jnp.zeros(seg_col.shape, jnp.int32), jnp.zeros(seg_row.shape, jnp.int32)
    for end in ends:
        col = col + (at_col >= end).astype(jnp.int32)
        row = row + (at_row >= end).astype(jnp.int32)
    seg_col[...] = col
    seg_row[...] = row


def key_range(ends, first, last, cases, total):
    low, high = jnp.int32(0), jnp.int32(total)
    for end in ends:
        low = jnp.maximum(low, jnp.where(end <= first, end, 0))
        high = jnp.minimum(high, jnp.where(end > last, end, total))
    start = lax.div(low, 128)
    need = lax.div(high + 127, 128) - start
    case, size = jnp.int32(0), jnp.int32(cases[0])
    for j in range(1, len(cases)):
        more = need > cases[j - 1]
        case = jnp.where(more, j, case)
        size = jnp.where(more, cases[j], size)
    start = jnp.minimum(start, total // 128 - size)
    return pl.multiple_of(start * 128, 128), case


def for_blocks(ends, total, rows_in_block, cases, block):
    cases = tuple(c for c in cases if c < total // 128) + (total // 128,)

    @pl.loop(0, total // rows_in_block)
    def _(i):
        first = i * rows_in_block
        start, case = key_range(ends, first, first + rows_in_block - 1, cases, total)
        for j, n in enumerate(cases):
            pl.when(case == j)(functools.partial(block, pl.multiple_of(first, rows_in_block), n, start))


def attend_kernel(len_ref, tok, w, vecs, qkv, ctx, lse, seg_col, seg_row, *, group, bq, cases, nseq):
    total = tok.shape[0]
    ends = seq_ends(len_ref, nseq)
    fill_segments(ends, seg_col, seg_row)
    for part in range(3):
        cols = pl.ds(part * GROUP, GROUP)
        made = dot(tok[...], w[:, cols])
        if part != 1:
            made = made + vecs[part // 2 : part // 2 + 1, pl.ds(group * GROUP, GROUP)]
        made = made.astype(BF)
        qkv[:, cols] = made * BF(1.0 / math.sqrt(HEAD_DIM)) if part == 0 else made

    def block(first, n, start):
        nk = n * 128
        rows, keys = pl.ds(first, bq), pl.ds(start, nk)
        same = jnp.concatenate([seg_col[rows, :]] * n, 1) == seg_row[0:1, keys]
        lane = lax.broadcasted_iota(jnp.int32, (bq, PAIR), 1)
        stats = jnp.zeros((bq, PAIR), F32)
        for pair in range(2):
            q = qkv[rows, pl.ds(pair * PAIR, PAIR)]
            k = qkv[keys, pl.ds(GROUP + pair * PAIR, PAIR)]
            v = qkv[keys, pl.ds(2 * GROUP + pair * PAIR, PAIR)]
            v_ones = jnp.concatenate([v, jnp.ones((nk, PAIR), BF)], 1)
            outs = []
            for h in range(2):
                s = dot(jnp.where((lane < HEAD_DIM) == (h == 0), q, BF(0)), k, 1, 1)
                s = jnp.where(same, s, MASKED)
                top = jnp.max(s, axis=1, keepdims=True)
                o = dot(jnp.exp2((s - top) * LOG2E).astype(BF), v_ones)
                norm = o[:, PAIR:]
                outs.append(o[:, :PAIR] * (1.0 / norm))
                stats = jnp.where(lane == pair * 2 + h, top * LOG2E + jnp.log2(norm), stats)
            ctx[rows, pl.ds(pair * PAIR, PAIR)] = jnp.where(lane < HEAD_DIM, outs[0], outs[1]).astype(BF)
        lse[:, rows] = stats.T[0:8, :]

    for_blocks(ends, total, bq, cases, block)


def attend(lens, tok, packed, group, vecs, after=(), bq=256, cases=(2, 3, 4, 5, 6)):
    total, width = tok.shape
    vmem = pl.BlockSpec(memory_space=pltpu.VMEM)
    return call(
        functools.partial(attend_kernel, group=group, bq=bq, cases=cases, nseq=lens.shape[1]),
        9,
        after,
        grid=(1,),
        in_specs=[
            pl.BlockSpec(memory_space=pltpu.SMEM),
            vmem,
            pl.BlockSpec((width, 3 * GROUP), lambda _: (0, group)),
            vmem,
        ],
        out_specs=[vmem] * 3,
        out_shape=[
            jax.ShapeDtypeStruct((total, 3 * GROUP), BF),
            jax.ShapeDtypeStruct((total, GROUP), BF),
            jax.ShapeDtypeStruct((8, total), F32),
        ],
        scratch_shapes=[pltpu.VMEM((total, 128), jnp.int32), pltpu.VMEM((8, total), jnp.int32)],
        name="attend",
    )(lens, tok, packed, vecs)


def attend_back_kernel(
    len_ref, core_ref, tok_t, out_w, qkv, ctx, lse_in, att_back, *refs, extra, carry, n_dw, bq, cases, nseq, chunk=2
):
    extras, carried, refs = refs[:extra], refs[extra : extra + carry], refs[extra + carry :]
    dw, (dqkv, sums) = refs[:n_dw], refs[n_dw : n_dw + 2]
    seg_col, seg_row, key_t, do, dk_sum, dv_sum, p_s, ds_s = refs[n_dw + 2 :]
    width, total = tok_t.shape
    ends = seq_ends(len_ref, nseq)
    fill_segments(ends, seg_col, seg_row)
    do[...] = dot(att_back[...], out_w[...], 1, 1).astype(BF)
    key_t[...] = qkv[:, pl.ds(GROUP, GROUP)].T
    dk_sum[...] = jnp.zeros_like(dk_sum)
    dv_sum[...] = jnp.zeros_like(dv_sum)
    head = lax.broadcasted_iota(jnp.int32, (8, GROUP), 1) // HEAD_DIM == lax.broadcasted_iota(jnp.int32, (8, GROUP), 0)
    head = head.astype(BF)

    def block(first, n, start):
        nk = n * 128
        rows, keys = pl.ds(first, bq), pl.ds(start, nk)
        seg_q = seg_row[0:1, rows]
        lane = lax.broadcasted_iota(jnp.int32, (bq, PAIR), 1)
        both = do[rows, :].astype(F32) * ctx[rows, :].astype(F32)
        high = both.astype(BF)
        low = (both - high.astype(F32)).astype(BF)
        delta = dot(head, high, 1, 1) + dot(head, low, 1, 1)
        lse = lse_in[:, rows]
        dqs = []
        for pair in range(2):
            cols = pl.ds(pair * PAIR, PAIR)
            k_cols, v_cols = pl.ds(GROUP + pair * PAIR, PAIR), pl.ds(2 * GROUP + pair * PAIR, PAIR)
            q, g = qkv[rows, cols], do[rows, cols]
            qs, gs = [], []
            for h in range(2):
                head_at = pair * 2 + h
                mine = (lane < HEAD_DIM) == (h == 0)
                qs.append(jnp.where(mine, q, BF(0)))
                gs.append(jnp.where(mine, g, BF(0)))
                for c in range(0, n, chunk):
                    wide = min(chunk, n - c) * 128
                    some = pl.ds(pl.multiple_of(start + c * 128, 128), wide)
                    s = dot(qkv[some, k_cols], qs[h], 1, 1)
                    same = jnp.concatenate([seg_col[some, :]] * (bq // 128), 1) == seg_q
                    p = jnp.exp2(jnp.where(same, s * LOG2E - lse[head_at : head_at + 1, :], MASKED))
                    dp = dot(qkv[some, v_cols], gs[h], 1, 1)
                    p_s[pl.ds(c * 128, wide), pl.ds(h * bq, bq)] = p.astype(BF)
                    ds_s[pl.ds(c * 128, wide), pl.ds(h * bq, bq)] = (p * (dp - delta[head_at : head_at + 1, :])).astype(BF)
            for h in range(2):
                dqs.append(dot(key_t[pl.ds((pair * 2 + h) * HEAD_DIM, HEAD_DIM), keys], ds_s[pl.ds(0, nk), pl.ds(h * bq, bq)]))
            dv_sum[keys, cols] += dot(p_s[pl.ds(0, nk), :], jnp.concatenate(gs, 0))
            dk_sum[keys, cols] += dot(ds_s[pl.ds(0, nk), :], jnp.concatenate(qs, 0))
        dqkv[rows, pl.ds(0, GROUP)] = (jnp.concatenate(dqs, 0).T * (1.0 / math.sqrt(HEAD_DIM))).astype(BF)

    for_blocks(ends, total, bq, cases, block)
    dqkv[:, pl.ds(GROUP, GROUP)] = dk_sum[...].astype(BF)
    dqkv[:, pl.ds(2 * GROUP, GROUP)] = dv_sum[...].astype(BF)
    d = dqkv[...]
    bias_sums = jnp.sum(d.astype(F32), axis=0, keepdims=True)
    sums[...] = jnp.broadcast_to(bias_sums, sums.shape)
    put_shares(dot(tok_t[...], d), core_ref[0, 0], dw, pl.ds(0, 3 * GROUP))
    for source, target in zip(carried, dw):
        target[..., pl.ds(3 * GROUP, width)] = source[...]
    if extra:
        *before, sums_one, sums_two, up_sums = extras
        query = jnp.concatenate([b[0:1, :GROUP] for b in before] + [bias_sums[:, :GROUP]], 1)
        value = jnp.concatenate([b[0:1, 2 * GROUP :] for b in before] + [bias_sums[:, 2 * GROUP :]], 1)
        rows = [query, value, sums_one[2:3], sums_one[0:1], sums_one[1:2], sums_two[2:3], sums_two[0:1], sums_two[1:2]]
        at = lax.broadcasted_iota(jnp.int32, (128, width), 0)
        table = jnp.zeros((128, width), F32)
        for j, row in enumerate([*rows, *(up_sums[j : j + 1] for j in range(4))]):
            table = jnp.where(at == j, row, table)
        put_shares(table.T, core_ref[0, 0], dw, pl.ds(3 * GROUP, 128))


def attend_back(
    lens, core, tok_t, out_up, group, qkv, ctx, lse, att_back, n, extras=(), carried=(), after=(), bq=256,
    cases=(2, 3, 4, 5, 6),
):
    width, total = tok_t.shape
    vmem, smem = pl.BlockSpec(memory_space=pltpu.VMEM), pl.BlockSpec(memory_space=pltpu.SMEM)
    dw = shares(width, 3 * GROUP + (128 if extras else 0) + (width if carried else 0), n)
    return call(
        functools.partial(
            attend_back_kernel, extra=len(extras), carry=len(carried), n_dw=len(dw), bq=bq, cases=cases, nseq=lens.shape[1]
        ),
        15,
        after,
        pinned=True,
        grid=(1,),
        in_specs=[
            smem,
            smem,
            vmem,
            pl.BlockSpec((GROUP, width), lambda _: (group, 0)),
        ]
        + [vmem] * (4 + len(extras) + len(carried)),
        out_specs=[vmem] * (len(dw) + 2),
        out_shape=[
            *dw,
            jax.ShapeDtypeStruct((total, 3 * GROUP), BF),
            jax.ShapeDtypeStruct((8, 3 * GROUP), F32),
        ],
        scratch_shapes=[
            pltpu.VMEM((total, 128), jnp.int32),
            pltpu.VMEM((8, total), jnp.int32),
            pltpu.VMEM((GROUP, total), BF),
            pltpu.VMEM((total, GROUP), BF),
            pltpu.VMEM((total, GROUP), F32),
            pltpu.VMEM((total, GROUP), F32),
            pltpu.VMEM((total, 2 * bq), BF),
            pltpu.VMEM((total, 2 * bq), BF),
        ],
        name="attend_back",
    )(lens, core, tok_t, out_up, qkv, ctx, lse, att_back, *extras, *carried)


def tokens_back_kernel(grad_in, w, *refs):
    *ds, grad = refs
    d = jnp.concatenate([r[...] for r in ds], 1)
    grad[...] = grad_in[...] + dot(d, w[:, : d.shape[1]], 1, 1)


def tokens_back(grad, packed, ds, after=(), rows=256):
    total, width = grad.shape
    at = lambda i: (i, 0)
    return call(
        tokens_back_kernel,
        8,
        after,
        placed=True,
        grid=(total // rows,),
        in_specs=[pl.BlockSpec((rows, width), at), pl.BlockSpec(packed.shape, lambda i: (0, 0))]
        + [pl.BlockSpec((rows, 3 * GROUP), at)] * len(ds),
        out_specs=pl.BlockSpec((rows, width), at),
        out_shape=jax.ShapeDtypeStruct((total, width), F32),
        name="tokens_back",
    )(grad, packed, *ds)


def row_mean(value):
    return jnp.sum(value, axis=-1, keepdims=True) * (1.0 / value.shape[-1])


def norm(value):
    center = value - row_mean(value)
    inverse = lax.rsqrt(row_mean(center * center) + EPSILON)
    return center * inverse, inverse


def norm_back(upstream, normed, inverse, gain):
    scaled = upstream * gain
    return inverse * (scaled - row_mean(scaled) - normed * row_mean(scaled * normed))


def add_rows(sums, first, pieces):
    at = lax.broadcasted_iota(jnp.int32, sums.shape, 0)
    made = jnp.zeros(sums.shape, F32)
    for j, piece in enumerate(pieces):
        made = jnp.where(at == j, jnp.sum(piece, axis=0, keepdims=True), made)

    @pl.when(first)
    def _():
        sums[...] = made

    @pl.when(jnp.logical_not(first))
    def _():
        sums[...] += made


ROOT = math.sqrt(2.0 / math.pi)


def lay_down(core, pieces, whole):
    if len(pieces) == 1:
        whole[...] = pieces[0][...]
        return
    half = len(pieces) // 2
    pairs, each = pieces[0].shape[:2]
    first = 0
    for mine, other in zip(pieces[:half], pieces[half:]):
        cols = pl.ds(first, mine.shape[-1])
        for e in range(pairs):
            a, b = mine[e], other[e]
            whole[pl.ds(2 * e * each, each), cols] = jnp.where(core == 0, a, b)
            whole[pl.ds((2 * e + 1) * each, each), cols] = jnp.where(core == 0, b, a)
        first += mine.shape[-1]


def down_specs(pieces, parts, at):
    if len(pieces) == 1:
        hidden, width = pieces[0].shape
        return [pl.BlockSpec((hidden // parts, width), lambda j: (at(j), 0))]
    return [pl.BlockSpec((p.shape[0] // parts, *p.shape[1:]), lambda j: (at(j), 0, 0)) for p in pieces]


def forward_kernel(core_ref, ctx0, ctx1, ctx2, tok, out_w, up, bias, vecs, out_grad_far, *refs, rows, parts, n_down, n_dw):
    pieces, dw, refs = refs[:n_down], refs[n_down : n_down + n_dw], refs[n_down + n_dw :]
    far, (slope, sums, act, total, down), near, (out_grad, sems) = refs[:6], refs[6:11], refs[11:17], refs[17:]
    normed, inverse, low, output, second, back_low = near
    bring = pltpu.make_async_copy(out_grad_far, out_grad, sems.at[6])
    take = [pltpu.make_async_copy(near[i], far[i], sems.at[i]) for i in range(6)]
    j = pl.program_id(0)
    width = tok.shape[1]
    blocks = tok.shape[0] // rows

    @pl.when(j == 0)
    def _():
        bring.start()

        @pl.loop(0, blocks)
        def _(i):
            at = pl.ds(pl.multiple_of(i * rows, rows), rows)
            ctx = jnp.concatenate([ctx0[at, :], ctx1[at, :], ctx2[at, :]], 1)
            n, r = norm(tok[at, :].astype(F32) + (dot(ctx, out_w[...]) + vecs[2:3, :]))
            normed[at, :] = n
            inverse[at, :] = jnp.broadcast_to(r, (rows, inverse.shape[1]))
            middle = n * vecs[3:4, :] + vecs[4:5, :]
            low[at, :] = middle.astype(BF)
            total[at, :] = middle + vecs[5:6, :]

        for copy in take[:3]:
            copy.start()

    @pl.when(j < parts)
    def _():
        x = dot(low[...], up[...]) + bias[...]
        w = ROOT + (ROOT * 0.044715) * (x * x)
        gate = 0.5 + 0.5 * jnp.tanh(x * w)
        made = x * gate
        slope[...] = (gate + made * (1.0 - gate) * (6.0 * w - 4.0 * ROOT)).astype(BF)
        act[j] = made.astype(BF)
        lay_down(core_ref[0, 0], pieces, down)
        total[...] += dot(act[j], down[...])

    @pl.when(j == parts - 1)
    def _():
        bring.wait()

        @pl.loop(0, blocks)
        def _(i):
            at = pl.ds(pl.multiple_of(i * rows, rows), rows)
            n, r = norm(total[at, :])
            output[at, :] = (n * vecs[6:7, :] + vecs[7:8, :]).astype(BF)
            upstream = out_grad[at, :].astype(F32)
            made = norm_back(upstream, n, r, vecs[6:7, :])
            second[at, :] = made
            rounded = made.astype(BF)
            back_low[at, :] = rounded
            add_rows(sums, i == 0, (upstream * n, upstream, rounded.astype(F32)))

        for copy in take[3:]:
            copy.start()

    @pl.when(j >= parts)
    def _():
        put_shares(dot(act[j - parts], back_low[...], 0, 0), core_ref[0, 0], dw)

    @pl.when(j == 2 * parts - 1)
    def _():
        for copy in take:
            copy.wait()


def forward(core, ctxs, tok, out_up, up_bias, down, vecs, out_grad, n, rows=256):
    total, width = tok.shape
    hidden = up_bias.shape[1]
    parts = hidden // width
    vmem = pl.BlockSpec(memory_space=pltpu.VMEM)
    first = lambda j: jnp.minimum(j, parts - 1)
    last = lambda j: jnp.maximum(j - parts, 0)
    dw = shares(hidden, width, n)
    hbm = pl.BlockSpec(memory_space=pl.ANY)
    wide = (total, width)
    kept = [(wide, F32), ((total, 128), F32), (wide, BF), (wide, BF), (wide, F32), (wide, BF)]
    return call(
        functools.partial(forward_kernel, rows=rows, parts=parts, n_down=len(down), n_dw=len(dw)),
        32,
        vmem=48,
        placed=True,
        pinned=True,
        grid=(2 * parts,),
        in_specs=[pl.BlockSpec(memory_space=pltpu.SMEM)]
        + [vmem] * 4
        + [
            pl.BlockSpec((width, width), lambda j: (0, 0)),
            pl.BlockSpec((width, width), lambda j: (0, first(j) + 1)),
            pl.BlockSpec((1, width), lambda j: (0, first(j))),
            vmem,
            hbm,
            *down_specs(down, parts, first),
        ],
        out_specs=down_specs(dw, parts, last)
        + [hbm] * len(kept)
        + [pl.BlockSpec((total, width), lambda j: (0, first(j))), vmem],
        out_shape=[
            *dw,
            *(jax.ShapeDtypeStruct(*k) for k in kept),
            jax.ShapeDtypeStruct((total, hidden), BF),
            jax.ShapeDtypeStruct((8, width), F32),
        ],
        scratch_shapes=[
            pltpu.VMEM((parts, total, width), BF),
            pltpu.VMEM((total, width), F32),
            pltpu.VMEM((width, width), BF),
            *(pltpu.VMEM(*k) for k in kept),
            pltpu.VMEM((total, width), BF),
            pltpu.SemaphoreType.DMA((7,)),
        ],
        name="forward",
    )(core, *ctxs, tok, out_up, out_up, up_bias, vecs, out_grad, *down)


def backward_kernel(
    core_ref, back_low, slope, low, up, vecs, *refs, rows, n_dw, n_down
):
    far, pieces, refs = refs[:6], refs[6 : 6 + n_down], refs[6 + n_down :]
    dw, out_dw, refs = refs[: n_dw[0]], refs[n_dw[0] : sum(n_dw)], refs[sum(n_dw) :]
    (up_sums, sums), out_far, (low_t, back, ex, down), near, (entry_grad, att_back, sems) = (
        refs[:2], refs[2:4], refs[4:8], refs[8:14], refs[14:]
    )
    second, normed, inverse, ctx0, ctx1, ctx2 = near
    bring = [pltpu.make_async_copy(far[i], near[i], sems.at[i]) for i in range(6)]
    take = [pltpu.make_async_copy(a, b, sems.at[6 + i]) for i, (a, b) in enumerate(zip((entry_grad, att_back), out_far))]
    j = pl.program_id(0)
    blocks = low.shape[0] // rows

    @pl.when(j == 0)
    def _():
        for copy in bring:
            copy.start()
        low_t[...] = low[...].T
        back[...] = jnp.zeros_like(back)

    lay_down(core_ref[0, 0], pieces, down)
    ex[...] = (dot(back_low[...], down[...], 1, 1) * slope[...].astype(F32)).astype(BF)
    up_sums[...] = jnp.broadcast_to(jnp.sum(ex[...].astype(F32), axis=0, keepdims=True), up_sums.shape)
    back[...] += dot(ex[...], up[...], 1, 1)
    put_shares(dot(low_t[...], ex[...]), core_ref[0, 0], dw)

    @pl.when(j == pl.num_programs(0) - 1)
    def _():
        for copy in bring:
            copy.wait()

        @pl.loop(0, blocks)
        def _(i):
            at = pl.ds(pl.multiple_of(i * rows, rows), rows)
            upstream = second[at, :] + back[at, :].astype(BF).astype(F32)
            n = normed[at, :]
            made = norm_back(upstream, n, inverse[at, 0:1], vecs[3:4, :])
            entry_grad[at, :] = made
            rounded = made.astype(BF)
            att_back[at, :] = rounded
            add_rows(sums, i == 0, (upstream * n, upstream, rounded.astype(F32)))

        for copy in take:
            copy.start()
        ctx = jnp.concatenate([ctx0[...], ctx1[...], ctx2[...]], 1)
        put_shares(dot(ctx, att_back[...], 0, 0), core_ref[0, 0], out_dw)
        for copy in take:
            copy.wait()


def backward(core, back_low, down, slope, low, out_up, second, normed, inverse, ctxs, vecs, n, after=(), rows=256):
    total, width = low.shape
    hidden = slope.shape[1]
    vmem = pl.BlockSpec(memory_space=pltpu.VMEM)
    dw, out_dw = shares(width, hidden, n), shares(width, width, n)
    hbm = pl.BlockSpec(memory_space=pl.ANY)
    lead = (0,) * (len(dw[0].shape) - 1)
    return call(
        functools.partial(backward_kernel, rows=rows, n_dw=(len(dw), len(out_dw)), n_down=len(down)),
        26,
        after,
        vmem=44,
        placed=True,
        pinned=True,
        grid=(hidden // width,),
        in_specs=[
            pl.BlockSpec(memory_space=pltpu.SMEM),
            vmem,
            pl.BlockSpec((total, width), lambda j: (0, j)),
            vmem,
            pl.BlockSpec((width, width), lambda j: (0, j + 1)),
            vmem,
        ]
        + [hbm] * 6
        + down_specs(down, hidden // width, lambda j: j),
        out_specs=[pl.BlockSpec((*d.shape[:-1], width), lambda j: (*lead, j)) for d in dw]
        + [vmem] * len(out_dw)
        + [pl.BlockSpec((8, width), lambda j: (0, j)), vmem, hbm, hbm],
        out_shape=[
            *dw,
            *out_dw,
            jax.ShapeDtypeStruct((8, hidden), F32),
            jax.ShapeDtypeStruct((8, width), F32),
            jax.ShapeDtypeStruct((total, width), F32),
            jax.ShapeDtypeStruct((total, width), BF),
        ],
        scratch_shapes=[
            pltpu.VMEM((width, total), BF),
            pltpu.VMEM((total, width), F32),
            pltpu.VMEM((total, width), BF),
            pltpu.VMEM((width, width), BF),
            pltpu.VMEM((total, width), F32),
            pltpu.VMEM((total, width), F32),
            pltpu.VMEM((total, 128), F32),
            *[pltpu.VMEM((total, GROUP), BF)] * 3,
            pltpu.VMEM((total, width), F32),
            pltpu.VMEM((total, width), BF),
            pltpu.SemaphoreType.DMA((8,)),
        ],
        name="backward",
    )(core, back_low, slope, low, out_up, vecs, second, normed, inverse, *ctxs, *down)


def pack_kernel(query, key, value, table, packed):
    own, width = query.shape
    for g in range(width // GROUP):
        for part, matrix in enumerate((query, key, value)):
            packed[:, pl.ds((3 * g + part) * GROUP, GROUP)] = matrix[:, pl.ds(g * GROUP, GROUP)]
    packed[:, pl.ds(3 * width, 128)] = table[...].astype(F32).T[:own, :].astype(BF)


def pack(query, key, value, rows):
    own, width = query.shape
    table = jnp.pad(rows, ((0, 128 - rows.shape[0]), (0, 128 - own)))
    vmem = pl.BlockSpec(memory_space=pltpu.VMEM)
    return call(
        pack_kernel,
        1,
        in_specs=[vmem] * 4,
        out_specs=vmem,
        out_shape=jax.ShapeDtypeStruct((own, 3 * width + 128), BF),
        name="pack",
    )(query, key, value, table)


def turn_kernel(packed, vecs):
    vecs[...] = packed[...].astype(F32).T[: vecs.shape[0], :]


def turn(packed, first):
    width = packed.shape[0]
    return call(
        turn_kernel,
        1,
        grid=(1,),
        in_specs=[pl.BlockSpec((width, 128), lambda _: (0, first // 128))],
        out_specs=pl.BlockSpec(memory_space=pltpu.VMEM),
        out_shape=jax.ShapeDtypeStruct((16, width), F32),
        name="turn",
    )(packed)


class Cube:
    def __init__(self, mesh):
        self.n_dp, self.n_fsdp = mesh.shape["dp"], mesh.shape["fsdp"]
        self.n = self.n_dp * self.n_fsdp
        self.bits = self.n.bit_length() - 1
        inner = self.n_fsdp.bit_length() - 1
        assert self.n == 1 << self.bits and self.n_fsdp == 1 << inner
        self.near = list(range(1, inner))
        self.far = list(range(inner, self.bits))

    def swap(self, value, bit):
        return lax.ppermute(value, AXES, [(i, i ^ (1 << bit)) for i in range(self.n)])

    def my_bit(self, bit):
        return (lax.axis_index(AXES) >> bit) & 1

    def join(self, mine, other, bit, done):
        at = sum(b > bit for b in done)
        last = self.my_bit(bit) == 1
        return jnp.stack([jnp.where(last, other, mine), jnp.where(last, mine, other)], at)

    def gather_near(self, piece, step, done):
        bit = self.near[::-1][step]
        return self.join(piece, self.swap(piece, bit), bit, done), [*done, bit]

    def halve(self, piece):
        half = piece.shape[-1] // 256 * 128
        return [piece[..., :half], piece[..., half:]]

    def gather_far(self, parts, step, done):
        orders = [self.far[::-1], self.far[:1] + self.far[:0:-1]]
        bits = [order[step] for order in orders]
        before = [[*done, *order[:step]] for order in orders]
        return [self.join(p, self.swap(p, bit), bit, d) for p, bit, d in zip(parts, bits, before)]

    def gather_core(self, parts, others):
        done = self.near + self.far
        whole = jnp.concatenate([self.join(p, o, 0, done) for p, o in zip(parts, others)], -1)
        return whole.reshape(-1, whole.shape[-1])

    def fold(self, part, left, bit):
        at = left.index(bit)
        rest = left[:at] + left[at + 1 :]
        mine = self.my_bit(bit)
        keep = lax.dynamic_index_in_dim(part, mine, at, keepdims=False)
        give = lax.dynamic_index_in_dim(part, 1 - mine, at, keepdims=False)
        total = keep.astype(F32) + self.swap(give, bit).astype(F32)
        return (total.astype(BF) if rest else total), rest

    def scatter_core(self, given):
        left = list(range(self.bits - 1, -1, -1))
        if len(given) == 2:
            keep, give = given
            part = (keep.astype(F32) + self.swap(give, 0).astype(F32)).astype(BF)
            part = part.reshape((2,) * (self.bits - 1) + part.shape[1:])
        else:
            whole = given[0].reshape((2,) * self.bits + (-1, given[0].shape[-1]))
            part, _ = self.fold(whole, left, 0)
        return part

    def scatter_far(self, parts, step):
        made = []
        for part, order in zip(parts, (self.far, self.far[1:] + self.far[:1])):
            left = [b for b in range(self.bits - 1, 0, -1) if b not in order[:step]]
            made.append(self.fold(part, left, order[step])[0])
        return made


class Flow:
    def __init__(self, cube, parts):
        self.cube, self.parts, self.left = cube, list(parts), list(range(cube.bits - 1, 0, -1))
        self.todo = [("far", i) for i in range(len(cube.far))] + [("near", bit) for bit in cube.near]

    def step(self, *after):
        if not self.todo:
            return
        (where, i), *self.todo = self.todo
        parts = [tie(p, *after) for p in self.parts] if after else self.parts
        if where == "far":
            self.parts = self.cube.scatter_far(parts, i)
        else:
            part = jnp.concatenate(parts, -1) if len(parts) > 1 else parts[0]
            left = [b for b in self.cube.near if b >= i][::-1]
            self.parts = [self.cube.fold(part, left, i)[0]]

    def finish(self):
        while self.todo:
            self.step()
        return self.parts[0]


def tie(value, *others):
    return lax.optimization_barrier((value, *others))[0]


def body(cube, *args):
    (
        tokens, seq_lengths, query_weight, query_bias, key_weight, value_weight, value_bias, out_weight, out_bias,
        first_gain, first_shift, up_weight, up_bias, down_weight, down_bias, second_gain, second_shift, out_grad,
    ) = args
    n = cube.n
    width = tokens.shape[1]
    own = width // n
    groups = width // GROUP
    hidden = up_weight.shape[1]
    each = hidden // width
    core = cube.my_bit(0).astype(jnp.int32).reshape(1, 1)

    vectors = (query_bias, value_bias, out_bias, first_gain, first_shift, down_bias, second_gain, second_shift)
    rows = jnp.concatenate([jnp.stack(vectors), up_bias.reshape(each, own)])
    piece, done = pack(query_weight, key_weight, value_weight, rows), []
    out_up = lax.all_gather(jnp.concatenate([out_weight, up_weight], 1), AXES, axis=0, tiled=True)
    down_piece, down_done = down_weight, []
    steps_near, steps_far = len(cube.near), len(cube.far)
    for step in range(steps_near):
        piece, done = cube.gather_near(piece, step, done)
    parts = cube.halve(piece)
    tok_t = tie(tokens, piece).T
    for step in range(max(steps_far, steps_near)):
        if step < steps_near:
            down_piece = tie(down_piece, *parts)
        if step < steps_far:
            parts = cube.gather_far(parts, step, done)
        if step < steps_near:
            down_piece, down_done = cube.gather_near(down_piece, step, down_done)
    packed = cube.gather_core(parts, [cube.swap(p, 0) for p in parts])
    vecs = turn(packed, 3 * GROUP * groups)

    down_parts = [tie(p, packed) for p in cube.halve(down_piece)]
    made, wait = [], [tok_t]
    for g in range(groups):
        if g < steps_far:
            down_parts = cube.gather_far(down_parts, g, down_done)
        made.append(attend(seq_lengths, tokens, packed, g, vecs, wait))
        wait = [made[-1][2], *down_parts]
        if g == 0:
            up_b = tie(vecs[8 : 8 + each], made[0][2])
            up_b = up_b.reshape(each, n, own).transpose(1, 0, 2).reshape(1, hidden)
        down_parts = [tie(p, made[-1][2]) for p in down_parts] if g < steps_far else down_parts
    for step in range(groups, steps_far):
        down_parts = cube.gather_far(down_parts, step, down_done)
    ctxs = [m[1] for m in made]
    down_others = [cube.swap(p, 0) for p in down_parts]
    if hidden // n % 16:
        down = [cube.gather_core(down_parts, down_others)]
    else:
        down = [p.reshape(-1, *p.shape[-2:]) for p in (*down_parts, *down_others)]
    *down_dw, normed, inverse, low, output, second, back_low, slope, sums_two = forward(
        core, ctxs, tokens, out_up, up_b, down, vecs, out_grad, n
    )
    down_flow = Flow(cube, cube.halve(cube.scatter_core(down_dw)))

    *dws, up_sums, sums_one, grad, att_back = backward(
        core, back_low, down, slope, low, out_up, second, normed, inverse, ctxs, vecs, n
    )
    half = len(dws) // 2
    out_dw = dws[half:]
    up_sums = up_sums[0].reshape(width, each).T
    wait = down_flow.parts
    down_flow.step(sums_one)
    flows = [down_flow, Flow(cube, cube.halve(cube.scatter_core(dws[:half])))]
    later, sums_qkv, ds = [], [], []
    for g in range(groups):
        qkv, ctx, lse = made[g]
        extras = (*sums_qkv, sums_one, sums_two, up_sums) if g == groups - 1 else ()
        *dw, d, sums = attend_back(
            seq_lengths, core, tok_t, out_up, g, qkv, ctx, lse, att_back, n, extras, out_dw if g == 0 else (), wait
        )
        ds.append(d)
        sums_qkv.append(sums)
        wait = [p for flow in flows for p in flow.parts]
        if g < groups - 1:
            for flow in flows:
                flow.step(sums)
        if g == groups - 1:
            dw = [tie(p, *(p for flow in flows for p in flow.parts)) for p in dw]
        if g == 0:
            flows.append(Flow(cube, [cube.scatter_core(dw)]))
        else:
            later.append(cube.scatter_core(dw))
    both = Flow(cube, later)
    grad = tokens_back(grad, packed, ds, later[-1:])
    while both.todo or any(flow.todo for flow in flows):
        before = [p for flow in (both, *flows) for p in flow.parts]
        for flow in (both, *flows):
            flow.step(*before)
    own_down, own_up, first = [flow.parts[0] for flow in flows]
    both = both.parts[0]
    owned = [first]
    owned += [both[:, g * 3 * GROUP : (g + 1) * 3 * GROUP + (128 if g == groups - 2 else 0)] for g in range(groups - 1)]
    own_out = owned[0][:, 3 * GROUP :]
    own_q, own_k, own_v = [
        jnp.concatenate([p[:, part * GROUP : (part + 1) * GROUP] for p in owned], 1) for part in range(3)
    ]
    own_vec = owned[-1][:, 3 * GROUP :]
    q_b, v_b, out_b, gain_one, shift_one, down_b, gain_two, shift_two = [own_vec[:, j] for j in range(8)]
    own_up_b = own_vec[:, 8 : 8 + each].reshape(-1)
    return (
        output, grad, own_q, q_b, own_k, own_v, v_b, own_out, out_b, gain_one, shift_one,
        own_up, own_up_b, own_down, down_b, gain_two, shift_two,
    )


def solution(mesh):
    both = P(AXES)
    rows = P(AXES, None)
    matrix, vector = rows, both
    in_specs = (
        rows, rows, matrix, vector, matrix, matrix, vector, matrix, vector, vector, vector,
        matrix, vector, matrix, vector, vector, vector, rows,
    )
    out_specs = (
        rows, rows, matrix, vector, matrix, matrix, vector, matrix, vector, vector, vector,
        matrix, vector, matrix, vector, vector, vector,
    )
    return jax.shard_map(
        functools.partial(body, Cube(mesh)), mesh=mesh, in_specs=in_specs, out_specs=out_specs, check_vma=False
    )
```
